32 devices in a mesh: groups: 2 (over y), section: 4 (over z), tp: 4 (over x, core).
Axes of the slice: x: 2, y: 2, z: 4, core: 2. Of those that a mesh axis runs over, the one named last changes fastest.
Arguments:
- tokens: bfloat16 [8192, 8192], P(('groups', 'section'), 'tp'), parts along dimension 0
- norm_gain: bfloat16 [8192], P('tp'), may hold values from 0.29882812 to 3
- kv_weight: bfloat16 [8192, 8, 256], P('tp'), may hold values from -0.015625 to 0.015625
- block_owner: int32 [64, 1], P('groups'), parts along dimension 0, may hold values from 0 to 3; in each aligned block of 8 rows (0 to 7, 8 to 15, ...) at most 4 rows name the same one
- resident_cache: bfloat16 [8, 256, 128, 256], P('tp', ('groups', 'section')), parts along dimension 1, may hold values from -5 to 5
- page_table: int32 [256, 8], P(('groups', 'section')), parts along dimension 0, may hold values from 0 to 47, as said below
- context_len: int32 [256], P(('groups', 'section')), parts along dimension 0, may hold values from 2 to 1024
- decode_query: bfloat16 [8, 256, 8, 128], P('tp', ('groups', 'section')), parts along dimension 1, may hold values from -30 to 30
- new_kv: bfloat16 [8, 256, 256], P('tp', ('groups', 'section')), parts along dimension 1, may hold values from -5 to 5
Outputs:
- decoded: float32 [8, 256, 8, 128], P('tp', ('groups', 'section')), parts along dimension 1
The draws below stay inside these ranges and needn't reach their ends.
There are 2 independent parts, one for each index of `groups`. The reference program is written for one: setup_inputs(seed, part) draws one part's arguments, and reference() takes and returns one part's arrays. A program takes and returns all parts, laid end to end along the dimension named above; an argument that names none is the same for every part. Nothing has to cross between parts.
Inputs may be any that keep to these rules, and one draw needn't show every extreme that they name: `block_owner`: within the 8 blocks of one prefill device no owner is named more than 4 times, a bound that some block reaches. `page_table`: column 0 of every request names a resident page (below 32), a different one for each request of one owner; the other columns name any page.
All inputs are finite; a program needn't handle non-finite values.
Results may differ from the reference program's by a relative error of at most 0.0016.
Values may be sent and summed in bfloat16 or wider, within the bound.
A program may use at most 192 MiB of HBM per device.

```python
import math
import jax
import jax.numpy as jnp
import numpy as np
from jax import lax

D = 8192
KVH = 8
HD = 128
BLOCK = 128
MAXP = 8
TOK_DEV = 1024
REQ = 32
POOL = 32
GQ = 8
NB = 8
CAP = 4
PAGES = 48
REQS = 128
N_SECTION = 4
N_TP = 4


def shared_pages(key):
    streams = jax.random.split(key, 5)

    def pick_first(stream_key):
        return jax.random.permutation(stream_key, POOL)[:REQ]
    first_page = jax.vmap(pick_first)(jax.random.split(streams[0], N_SECTION)).astype(jnp.int32)
    later_pages = jax.random.randint(streams[1], (N_SECTION, REQ, MAXP - 1), 0, PAGES).astype(jnp.int32)
    aligned = jax.random.randint(streams[2], (N_SECTION, REQ), 0, 2).astype(jnp.int32)
    strength = jax.random.uniform(streams[3], (N_SECTION, REQ, KVH), minval=12.0, maxval=30.0)
    signs = (jax.random.randint(streams[4], (N_SECTION, REQ, KVH, HD), 0, 2) * 2 - 1).astype(jnp.float32)
    return (first_page, later_pages, aligned, strength, signs)


def draw_page_table(key, part):
    shared = shared_pages(key)
    table = jnp.concatenate([shared[0][:, :, None], shared[1]], axis=2)
    return table.reshape(N_SECTION * REQ, MAXP)


def draw_resident_cache(key, part):
    key = jax.random.fold_in(key, 5)
    shape = (KVH, N_SECTION, POOL, BLOCK, 2 * HD)
    base = jnp.clip(jax.random.normal(key, shape), -5.0, 5.0)
    return base.reshape(KVH, N_SECTION * POOL, BLOCK, 2 * HD).astype(jnp.bfloat16)


def draw_decode_query(key, part):
    key = jax.random.fold_in(key, 7)
    shape = (KVH, N_SECTION, REQ, GQ, HD)
    base = jnp.clip(2.0 * jax.random.normal(key, shape), -8.0, 8.0)
    return base.reshape(KVH, N_SECTION * REQ, GQ, HD).astype(jnp.bfloat16)


def draw_tokens(key, part):
    key = jax.random.fold_in(key, 9)
    streams = jax.random.split(key, 3)
    rows_all = N_SECTION * TOK_DEV
    ramp = jnp.arange(D, dtype=jnp.float32) / (D - 1)
    base = jnp.clip(jax.random.normal(streams[0], (rows_all, D)), -4.0, 4.0)
    row_scale = jnp.exp(jax.random.uniform(streams[1], (rows_all,), minval=0.0, maxval=math.log(10.0)))
    col_scale = jnp.exp(jax.random.uniform(streams[2], (D,), minval=0.0, maxval=math.log(10.0)) + 0.5 * math.log(3.0) * ramp)
    return (base * row_scale[:, None] * col_scale[None, :]).astype(jnp.bfloat16)


def with_ends(array, key, low, high):
    place = [jax.random.randint(jax.random.fold_in(key, axis), (), 0, length) for axis, length in enumerate(array.shape)]
    longest = array.shape.index(max(array.shape))
    next_to = place[:longest] + [(place[longest] + 1) % array.shape[longest]] + place[longest + 1:]
    return array.at[tuple(place)].set(low).at[tuple(next_to)].set(high)


def block_levels(rng, shape, cuts, smallest, high):
    level, own = 1.0, jax.random.fold_in(rng, 6)
    for position, blocks in cuts:
        draws = jnp.exp(jax.random.uniform(jax.random.fold_in(own, position), (blocks,), jnp.float32, smallest / len(cuts), high / len(cuts)))
        level = level * jnp.repeat(draws, shape[position] // blocks).reshape([-1 if axis == position else 1 for axis in range(len(shape))])
    return level


def routed_block(rng, own, number, rows, count, top, limit, lean):
    order = jax.random.permutation(rng, count)
    heavy_load, ordinary = portions_of(count, rows * top, limit, lean, True), portions_of(count, rows * top, limit, lean, False)
    places = jnp.arange(count)

    def named(sizes, rotation):
        used = int((sizes > 0).sum())
        fixed = max(1, used // 4)
        moved = fixed + (places - fixed + rotation * (used - fixed)) % max(1, count - fixed)
        return jnp.zeros((count,), jnp.int32).at[order[jnp.where(places < fixed, places, moved)]].set(jnp.asarray(sizes, jnp.int32))

    sizes = jnp.where(number % 4 == 0, named(heavy_load, number // 4), named(ordinary, number - number // 4 - 1))
    mixed = jax.random.permutation(jax.random.fold_in(own, 3), count)
    source_of, receiver = mixed[0:count // 2 * 2:2], mixed[1:count // 2 * 2:2]
    margin = jnp.minimum(sizes[source_of] - 1, limit - sizes[receiver]) // 2
    margin = jnp.where((source_of == order[0]) | (receiver == order[0]) | (sizes[receiver] == 0), 0, jnp.maximum(margin, 0))
    moved = jax.random.randint(jax.random.fold_in(own, 4), (count // 2,), 0, 1 << 20) % (margin + 1)
    sizes = sizes.at[source_of].add(-moved).at[receiver].add(moved)
    labels = jnp.searchsorted(jnp.cumsum(sizes), jnp.arange(rows * top), side="right").astype(jnp.int32)
    grid = labels.reshape(top, rows).T
    grid = grid[jax.random.permutation(jax.random.fold_in(own, 1), rows)]
    rotation = jax.random.randint(jax.random.fold_in(own, 2), (rows, 1), 0, top)
    return jnp.take_along_axis(grid, (jnp.arange(top)[None, :] + rotation) % top, axis=1)


def portions_of(amount, total, limit, slope, full):
    weights = [(1 << 20) // math.isqrt(rank ** slope) + 1 for rank in range(1, amount + 1)]
    largest = limit if full else min(limit, max(-(-total // amount), total * weights[0] // sum(weights)))
    least = 1 if total - largest >= amount - 1 else 0
    counts, surplus = [largest] + [least] * (amount - 1), total - largest - least * (amount - 1)
    while surplus > 0:
        movable = [i for i in range(1, amount) if counts[i] < largest] or [i for i in range(1, amount) if counts[i] < limit]
        mass, left = sum([weights[i] for i in movable]), surplus
        for i in movable:
            more = min(limit - counts[i], max(1, left * weights[i] // mass), surplus)
            counts[i] = counts[i] + more
            surplus = surplus - more
    return np.array(counts)


def normal_values(own_key, shape, spread, most, cuts=(), held_as=jnp.bfloat16):
    level = block_levels(own_key, shape, cuts, -0.22, 0.18) if cuts else 1.0
    array = jax.random.normal(own_key, shape, jnp.float32) * spread * level
    return jnp.minimum(jnp.maximum(array, -most), most).astype(held_as)


def setup_inputs(seed: int = 0, part: int = 0) -> dict:
    arg_keys = jax.random.split(jax.random.key(seed), 10)
    part_keys = jax.random.split(jax.random.fold_in(arg_keys[9], part), 10)
    tokens = draw_tokens(jax.random.fold_in(jax.random.fold_in(arg_keys[9], part), 71), part)
    norm_gain = jnp.clip(jnp.exp(math.log(3.0) - 2.306499 * jax.random.uniform(arg_keys[1], (D,), jnp.float32) ** block_levels(arg_keys[1], (D,), ((0, 4),), -0.2, 0.2)), 0.29882812, 3.0).astype(jnp.bfloat16)
    kv_weight = normal_values(arg_keys[2], (D, KVH, 2 * HD), (16 * D) ** -0.5, 0.015625, ((0, 4),))
    block_owner_keys = jax.random.split(jax.random.fold_in(part_keys[3], 1), (N_SECTION * NB) // NB)
    block_owner_turns = jax.random.permutation(jax.random.fold_in(part_keys[3], 3), (N_SECTION * NB) // NB)
    block_owner = jax.vmap(lambda own, number: routed_block(jax.random.fold_in(part_keys[3], 2), own, number, NB, N_SECTION, 1, CAP, 2))(block_owner_keys, block_owner_turns).reshape((N_SECTION * NB, 1))
    resident_cache = draw_resident_cache(jax.random.fold_in(jax.random.fold_in(arg_keys[9], part), 71), part)
    page_table = draw_page_table(jax.random.fold_in(jax.random.fold_in(arg_keys[9], part), 71), part)
    context_len = with_ends(jax.random.randint(part_keys[6], (REQS,), 2, MAXP * BLOCK + 1), jax.random.fold_in(part_keys[6], 1), 2, MAXP * BLOCK).astype(jnp.int32)
    decode_query = draw_decode_query(jax.random.fold_in(jax.random.fold_in(arg_keys[9], part), 71), part)
    new_kv = normal_values(part_keys[8], (KVH, REQS, 2 * HD), 1.0, 5.0, ((0, 4), (1, 4)))
    return {"tokens": tokens, "norm_gain": norm_gain, "kv_weight": kv_weight, "block_owner": block_owner, "resident_cache": resident_cache, "page_table": page_table, "context_len": context_len, "decode_query": decode_query, "new_kv": new_kv}


EPSILON = 1e-05

def block_ranks(owner_grid):
    blocks_dev = owner_grid.shape[1]
    same_owner = owner_grid[:, :, None] == owner_grid[:, None, :]
    positions = jnp.arange(blocks_dev, dtype=jnp.int32)
    earlier = positions[None, :] < positions[:, None]
    return lax.optimization_barrier(jnp.sum((same_owner & earlier[None]).astype(jnp.int32), axis=2))

def project_keyvals(tokens, norm_gain, kv_weight):
    widths = D // N_TP
    widened = tokens.astype(jnp.float32)
    squares = lax.optimization_barrier(jnp.sum(widened * widened, axis=1))
    normed = (widened * norm_gain.astype(jnp.float32)[None, :]).astype(jnp.bfloat16)
    flat_weight = kv_weight.reshape(D, KVH * 2 * HD)
    summed = jnp.zeros((tokens.shape[0], KVH * 2 * HD), jnp.float32)
    for device in range(N_TP):
        partial_sum = jnp.dot(normed[:, device * widths:(device + 1) * widths], flat_weight[device * widths:(device + 1) * widths], preferred_element_type=jnp.float32)
        rounded = lax.optimization_barrier(partial_sum.astype(jnp.bfloat16))
        summed = summed + rounded.astype(jnp.float32)
    scaled = summed * lax.rsqrt(squares / D + EPSILON)[:, None]
    keyval = scaled.astype(jnp.bfloat16).reshape(tokens.shape[0], KVH, 2 * HD)
    return jnp.transpose(keyval, (1, 0, 2))

def attend(page_pool, table, lengths, queries, fresh):
    heads_all, requests, group_size, head_dim = queries.shape
    length = table.shape[1] * page_pool.shape[2]
    gathered = page_pool[:, table].reshape(heads_all, requests, length, 2 * head_dim)
    cache_keys = gathered[..., :head_dim].astype(jnp.float32)
    cache_values = gathered[..., head_dim:].astype(jnp.float32)
    query_wide = queries.astype(jnp.float32)
    fresh_wide = fresh.astype(jnp.float32)
    score_scale = 1.0 / math.sqrt(head_dim)
    scores = jnp.einsum('hrgd,hrld->hrgl', query_wide, cache_keys) * score_scale
    own_score = jnp.einsum('hrgd,hrd->hrg', query_wide, fresh_wide[..., :head_dim]) * score_scale
    positions = jnp.arange(length, dtype=jnp.int32)
    live_mask = (positions[None, :] < lengths[:, None])[None, :, None, :]
    masked = jnp.where(live_mask, scores, jnp.float32(-1e+30))
    row_max = jnp.maximum(lax.optimization_barrier(jnp.max(masked, axis=3)), own_score)
    weights = jnp.where(live_mask, jnp.exp(masked - row_max[..., None]), jnp.float32(0.0))
    own_weight = jnp.exp(own_score - row_max)
    denominator = lax.optimization_barrier(jnp.sum(weights, axis=3)) + own_weight
    weights_low = lax.optimization_barrier(weights.astype(jnp.bfloat16)).astype(jnp.float32)
    own_low = lax.optimization_barrier(own_weight.astype(jnp.bfloat16)).astype(jnp.float32)
    mixed = jnp.einsum('hrgl,hrld->hrgd', weights_low, cache_values)
    mixed = mixed + own_low[..., None] * fresh_wide[:, :, None, head_dim:]
    return mixed / denominator[..., None]

def reference(tokens, norm_gain, kv_weight, block_owner, resident_cache, page_table, context_len, decode_query, new_kv):
    keyval = project_keyvals(tokens, norm_gain, kv_weight)
    blocks = keyval.reshape(KVH, N_SECTION * NB, BLOCK, 2 * HD)
    padded = jnp.concatenate([blocks, jnp.zeros((KVH, 1, BLOCK, 2 * HD), jnp.bfloat16)], axis=1)
    owner_flat = block_owner[:, 0]
    rank_flat = block_ranks(owner_flat.reshape(N_SECTION, NB)).reshape(-1)
    source = jnp.arange(N_SECTION * NB, dtype=jnp.int32) // NB
    block_ids = jnp.arange(N_SECTION * NB, dtype=jnp.int32)

    def one_owner(owner):
        slot = jnp.where(owner_flat == owner, source * CAP + rank_flat, N_SECTION * CAP).astype(jnp.int32)
        slot_source = jnp.full((N_SECTION * CAP,), N_SECTION * NB, dtype=jnp.int32).at[slot].set(block_ids, mode='drop')
        arrived = padded[:, slot_source]
        resident = lax.dynamic_slice_in_dim(resident_cache, owner * POOL, POOL, 1)
        page_pool = jnp.concatenate([resident, arrived], axis=1)
        table = lax.dynamic_slice_in_dim(page_table, owner * REQ, REQ, 0)
        lengths = lax.dynamic_slice_in_dim(context_len, owner * REQ, REQ, 0)
        queries = lax.dynamic_slice_in_dim(decode_query, owner * REQ, REQ, 1)
        fresh = lax.dynamic_slice_in_dim(new_kv, owner * REQ, REQ, 1)
        return attend(page_pool, table, lengths, queries, fresh)
    outputs = lax.map(one_owner, jnp.arange(N_SECTION, dtype=jnp.int32))
    return jnp.transpose(outputs, (1, 0, 2, 3, 4)).reshape(KVH, N_SECTION * REQ, GQ, HD)
```

```python
import functools
import math

import jax
import jax.numpy as jnp
from jax import lax
from jax.experimental import pallas as pl
from jax.experimental.pallas import tpu as pltpu
from jax.sharding import PartitionSpec as P

D = 8192


EPSILON = 1e-05
NEG = -1e30
GROUP = 4
MESH = pl.DeviceIdType.MESH


def block_ranks(owner_grid):
    blocks_dev = owner_grid.shape[1]
    same_owner = owner_grid[:, :, None] == owner_grid[:, None, :]
    positions = jnp.arange(blocks_dev, dtype=jnp.int32)
    earlier = positions[None, :] < positions[:, None]
    return jnp.sum((same_owner & earlier[None]).astype(jnp.int32), axis=2)


def page_counts(table, lengths, owner_flat, sections, pool, block, group_size):
    blocks_dev = owner_flat.shape[0] // sections
    slots_peer = 2 * ((blocks_dev + sections - 1) // sections)
    rank = block_ranks(owner_flat.reshape(sections, blocks_dev)).reshape(-1)
    ids = jnp.arange(owner_flat.shape[0], dtype=jnp.int32)
    placed = jnp.where(
        owner_flat == lax.axis_index("section"), pool + ids // blocks_dev * slots_peer + rank, -1
    )
    pages = jnp.concatenate([jnp.arange(pool, dtype=jnp.int32), placed])
    columns = jnp.repeat(table.T, group_size, axis=1)
    length = jnp.repeat(lengths, group_size)[None]
    begin = jnp.arange(columns.shape[0], dtype=jnp.int32)[:, None] * block
    whole = begin + block <= length
    partial = (begin < length) & ~whole
    same = pages[:, None, None] == columns[None]
    full = jnp.sum((same & whole[None]).astype(jnp.float32), axis=1)
    edge = jnp.sum((same & partial[None]).astype(jnp.float32), axis=1)
    rest = (length % block).astype(jnp.float32)
    zeros = length.astype(jnp.float32) - jnp.sum(full * block + edge * rest, axis=0, keepdims=True)
    misc = jnp.concatenate([rest, zeros, jnp.zeros((6, rest.shape[1]), jnp.float32)], axis=0)
    return full, edge, misc


def kernel(
    sections, tp, heads, block, chunk,
    part_ref, sq_ref, query_ref, cache_ref, fresh_ref, full_ref, edge_ref, aux_ref,
    out_ref,
    sib, cross_out, cross_in, sq_in, query_in, aux_in, kv, pages, scores, acc, res_acc,
    back_out, back_in, stat_out, stat_in, own_acc,
    sib_s, sib_r, cross_s, cross_r, sq_s, sq_r, query_s, query_r, aux_s, aux_r,
    back_s, back_r, stat_s, stat_r, page_s,
):
    me = lax.axis_index("section")
    t = lax.axis_index("tp")
    core, x = lax.rem(t, 2), lax.div(t, 2)
    chips = tp // 2
    rows = part_ref.shape[1]
    chunks = rows // chunk
    cols = query_ref.shape[1]
    dim = query_ref.shape[2]
    pool = cache_ref.shape[1]
    blocks_dev = rows // block
    scale = 1.0 / math.sqrt(dim)

    barrier = pltpu.get_barrier_semaphore()
    for d in range(1, tp):
        pl.semaphore_signal(
            barrier, inc=1, device_id={"tp": lax.rem(t + d, tp)}, device_id_type=MESH
        )
    for d in range(1, sections):
        pl.semaphore_signal(
            barrier, inc=1, device_id={"section": lax.rem(me + d, sections)}, device_id_type=MESH
        )
    pl.semaphore_wait(barrier, tp + sections - 2)

    def span(i):
        return pl.ds(pl.multiple_of(i * chunk, chunk), chunk)

    def sib_copy(d, i):
        group = lax.rem(x + d, chips) * 2 + 1 - core
        return pltpu.make_async_remote_copy(
            src_ref=part_ref.at[pl.ds(group * heads, heads), span(i)],
            dst_ref=sib.at[d, :, span(i)],
            send_sem=sib_s.at[d, i],
            recv_sem=sib_r.at[d, i],
            device_id={"tp": x * 2 + 1 - core},
            device_id_type=MESH,
        )

    def cross_copy(d, i):
        return pltpu.make_async_remote_copy(
            src_ref=cross_out.at[d - 1, :, span(i)],
            dst_ref=cross_in.at[d - 1, :, span(i)],
            send_sem=cross_s.at[d - 1, i],
            recv_sem=cross_r.at[d - 1, i],
            device_id={"tp": lax.rem(x + d, chips) * 2 + core},
            device_id_type=MESH,
        )

    def sq_copy(d):
        return pltpu.make_async_remote_copy(
            src_ref=sq_ref,
            dst_ref=sq_in.at[d - 1],
            send_sem=sq_s.at[d - 1],
            recv_sem=sq_r.at[d - 1],
            device_id={"tp": lax.rem(t + d, tp)},
            device_id_type=MESH,
        )

    def query_copy(d):
        return pltpu.make_async_remote_copy(
            src_ref=query_ref,
            dst_ref=query_in.at[d - 1],
            send_sem=query_s.at[d - 1],
            recv_sem=query_r.at[d - 1],
            device_id={"section": lax.rem(me + d, sections)},
            device_id_type=MESH,
        )

    def aux_copy(d):
        peer = lax.rem(me + d, sections)
        return pltpu.make_async_remote_copy(
            src_ref=aux_ref.at[peer],
            dst_ref=aux_in.at[d - 1],
            send_sem=aux_s.at[d - 1],
            recv_sem=aux_r.at[d - 1],
            device_id={"section": peer},
            device_id_type=MESH,
        )

    def back_copy(d):
        return pltpu.make_async_remote_copy(
            src_ref=back_out.at[d - 1],
            dst_ref=back_in.at[d - 1],
            send_sem=back_s.at[d - 1],
            recv_sem=back_r.at[d - 1],
            device_id={"section": lax.rem(me + sections - d, sections)},
            device_id_type=MESH,
        )

    def stat_copy(d):
        return pltpu.make_async_remote_copy(
            src_ref=stat_out.at[d - 1],
            dst_ref=stat_in.at[d - 1],
            send_sem=stat_s.at[d - 1],
            recv_sem=stat_r.at[d - 1],
            device_id={"section": lax.rem(me + sections - d, sections)},
            device_id_type=MESH,
        )

    def page_copy():
        return pltpu.make_async_copy(cache_ref, pages, page_s)

    for d in range(1, chips):
        for i in range(chunks):
            sib_copy(d, i).start()
    for d in range(1, tp):
        sq_copy(d).start()
    page_copy().start()
    for i in range(chunks):
        sib_copy(0, i).start()
    for d in range(1, sections):
        query_copy(d).start()
        aux_copy(d).start()

    for d in range(1, chips):
        group = lax.rem(x + d, chips) * 2 + core
        for i in range(chunks):
            sib_copy(d, i).wait_recv()
            mine = part_ref[pl.ds(group * heads, heads), span(i)]
            theirs = sib[d, :, span(i)]
            cross_out[d - 1, :, span(i)] = (
                mine.astype(jnp.float32) + theirs.astype(jnp.float32)
            ).astype(jnp.bfloat16)
            cross_copy(d, i).start()

    position = lax.broadcasted_iota(jnp.int32, (block, cols), 0).astype(jnp.float32)

    def attend(query, load, count_rows, rest, n_pages, extra=None, zeros=None):
        inside = position < rest

        def count(p):
            full, edge = count_rows(p)
            return full + jnp.where(inside, edge, 0.0)

        def first(step, top):
            base = step * GROUP
            for k in range(GROUP):
                keys = load(base + k)[:, :dim]
                s = lax.dot_general(
                    keys, query, (((1,), (1,)), ((), ())), preferred_element_type=jnp.float32
                ) * scale
                s = jnp.where(count(base + k) > 0, s, NEG)
                scores[pl.ds(pl.multiple_of((base + k) * block, block), block)] = s
                top = jnp.maximum(top, jnp.max(s.reshape(block // 8, 8, cols), axis=0))
            return top

        top = lax.fori_loop(0, n_pages // GROUP, first, jnp.full((8, cols), NEG, jnp.float32))
        top = jnp.max(top, axis=0, keepdims=True)
        if extra is not None:
            fresh = extra
            requests = fresh.shape[0]
            own = (
                lax.broadcasted_iota(jnp.int32, (requests, cols), 0) * (cols // requests)
            )
            column = lax.broadcasted_iota(jnp.int32, (requests, cols), 1)
            own = (column >= own) & (column < own + cols // requests)
            s_own = lax.dot_general(
                fresh[:, :dim], query, (((1,), (1,)), ((), ())), preferred_element_type=jnp.float32
            ) * scale
            s_own = jnp.where(own, s_own, NEG)
            top = jnp.maximum(top, jnp.max(s_own, axis=0, keepdims=True))
            top = jnp.maximum(top, jnp.where(zeros > 0, 0.0, NEG))
            w_own = jnp.where(own, jnp.exp(s_own - top), 0.0)
            acc[...] = lax.dot_general(
                fresh[:, dim:], w_own.astype(jnp.bfloat16), (((0,), (0,)), ((), ())),
                preferred_element_type=jnp.float32,
            )
            total = jnp.sum(w_own, axis=0, keepdims=True)
            total = total + jnp.where(zeros > 0, zeros * jnp.exp(0.0 - top), 0.0)
        else:
            acc[...] = jnp.zeros_like(acc)
            total = jnp.zeros((1, cols), jnp.float32)

        def second(step, total8):
            base = step * GROUP
            values, lows = [], []
            for k in range(GROUP):
                s = scores[pl.ds(pl.multiple_of((base + k) * block, block), block)]
                w = jnp.exp(s - top)
                c = count(base + k)
                total8 = total8 + jnp.sum((w * c).reshape(block // 8, 8, cols), axis=0)
                low = w.astype(jnp.bfloat16).astype(jnp.float32) * c
                lows.append(low.astype(jnp.bfloat16))
                values.append(load(base + k)[:, dim:])
            acc[...] += lax.dot_general(
                jnp.concatenate(values, axis=0), jnp.concatenate(lows, axis=0),
                (((0,), (0,)), ((), ())), preferred_element_type=jnp.float32,
            )
            return total8

        total8 = lax.fori_loop(0, n_pages // GROUP, second, jnp.zeros((8, cols), jnp.float32))
        return top, total + jnp.sum(total8, axis=0, keepdims=True)

    page_copy().wait()
    rest_own = aux_ref[0, 2 * blocks_dev : 2 * blocks_dev + 1, :]
    zeros_own = aux_ref[0, 2 * blocks_dev + 1 : 2 * blocks_dev + 2, :]
    res_stats = []
    for h in range(heads):
        stat = attend(
            query_ref[h],
            lambda p, h=h: pages[h, p],
            lambda p: (full_ref[pl.ds(p, 1), :], edge_ref[pl.ds(p, 1), :]),
            rest_own,
            pool,
            fresh_ref[h],
            zeros_own,
        )
        res_stats.append(stat)
        res_acc[h] = acc[...]

    for d in range(1, tp):
        sq_copy(d).wait_recv()
    squares = sq_ref[...]
    for d in range(1, tp):
        squares = squares + sq_in[d - 1]
    inverse = lax.rsqrt(squares / D + EPSILON)
    diagonal = lax.broadcasted_iota(jnp.int32, (block, block), 0) == lax.broadcasted_iota(
        jnp.int32, (block, block), 1
    )
    per_chunk = chunk // block
    for i in range(chunks):
        sib_copy(0, i).wait_recv()
        for d in range(1, chips):
            cross_copy(d, i).wait_recv()
        for k in range(per_chunk):
            j = i * per_chunk + k
            lanes = inverse[j : j + 1, :]
            factor = jnp.sum(
                jnp.where(diagonal, jnp.broadcast_to(lanes, (block, block)), 0.0),
                axis=1,
                keepdims=True,
            )
            at = slice(j * block, (j + 1) * block)
            for h in range(heads):
                value = part_ref[t * heads + h, at].astype(jnp.float32) + sib[0, h, at].astype(
                    jnp.float32
                )
                for d in range(1, chips):
                    value = value + cross_in[d - 1, h, at].astype(jnp.float32)
                kv[h, at] = (value * factor).astype(jnp.bfloat16)

    def load_block(h):
        return lambda p: kv[h, pl.ds(pl.multiple_of(p * block, block), block)]

    def serve(d, carry):
        query_copy(d).wait_recv()
        aux_copy(d).wait_recv()
        for h in range(heads):
            top, total = attend(
                query_in[d - 1, h],
                load_block(h),
                lambda p: (
                    aux_in[d - 1, pl.ds(p, 1), :],
                    aux_in[d - 1, pl.ds(blocks_dev + p, 1), :],
                ),
                aux_in[d - 1, 2 * blocks_dev : 2 * blocks_dev + 1, :],
                blocks_dev,
            )
            back_out[d - 1, h] = acc[...].astype(jnp.bfloat16)
            stat_out[d - 1, h] = jnp.concatenate(
                [top, total, jnp.zeros((6, cols), jnp.float32)], axis=0
            )
        back_copy(d).start()
        stat_copy(d).start()
        return carry

    lax.fori_loop(1, sections, serve, 0)
    own_stats = []
    for h in range(heads):
        stat = attend(
            query_ref[h],
            load_block(h),
            lambda p: (
                aux_ref[me, pl.ds(p, 1), :],
                aux_ref[me, pl.ds(blocks_dev + p, 1), :],
            ),
            rest_own,
            blocks_dev,
        )
        own_stats.append(stat)
        own_acc[h] = acc[...]

    for d in range(1, sections):
        back_copy(d).wait_recv()
        stat_copy(d).wait_recv()
    for h in range(heads):
        tops = [res_stats[h][0], own_stats[h][0]]
        totals = [res_stats[h][1], own_stats[h][1]]
        for d in range(1, sections):
            tops.append(stat_in[d - 1, h, 0:1, :])
            totals.append(stat_in[d - 1, h, 1:2, :])
        top = functools.reduce(jnp.maximum, tops)
        factors = [jnp.exp(one - top) for one in tops]
        total = sum(f * one for f, one in zip(factors, totals))
        mixed = res_acc[h] * factors[0] + own_acc[h] * factors[1]
        for d in range(1, sections):
            mixed = mixed + back_in[d - 1, h].astype(jnp.float32) * factors[d + 1]
        out_ref[h] = jnp.transpose(mixed / total)

    for d in range(chips):
        for i in range(chunks):
            sib_copy(d, i).wait_send()
            if d:
                cross_copy(d, i).wait_send()
    for d in range(1, tp):
        sq_copy(d).wait_send()
    for d in range(1, sections):
        query_copy(d).wait_send()
        aux_copy(d).wait_send()
        back_copy(d).wait_send()
        stat_copy(d).wait_send()


def per_device(
    sections,
    tp,
    tokens,
    norm_gain,
    kv_weight,
    block_owner,
    resident_cache,
    page_table,
    context_len,
    decode_query,
    new_kv,
):
    heads, pool, block, lanes = resident_cache.shape
    _, requests, group_size, dim = decode_query.shape
    cols = requests * group_size
    rows = tokens.shape[0]
    blocks_dev = rows // block
    chunk = min(rows, 256)
    chunks = rows // chunk
    chips = tp // 2
    widened = tokens.astype(jnp.float32)
    squares = jnp.sum(widened * widened, axis=1).reshape(blocks_dev, block)
    normed = (widened * norm_gain.astype(jnp.float32)[None, :]).astype(jnp.bfloat16)
    part = jnp.einsum(
        "td,dhc->htc", normed, kv_weight, preferred_element_type=jnp.float32
    ).astype(jnp.bfloat16)
    full, edge, misc = page_counts(
        page_table, context_len, block_owner[:, 0], sections, pool, block, group_size
    )
    aux = jnp.concatenate(
        [
            full[pool:].reshape(sections, blocks_dev, cols),
            edge[pool:].reshape(sections, blocks_dev, cols),
            jnp.broadcast_to(misc[None], (sections, 8, cols)),
        ],
        axis=1,
    )
    aux_rows = aux.shape[1]
    vmem = pl.BlockSpec(memory_space=pltpu.VMEM)
    dma = pltpu.SemaphoreType.DMA
    peers = sections - 1
    bf16, f32 = jnp.bfloat16, jnp.float32
    out = pl.pallas_call(
        functools.partial(kernel, sections, tp, heads, block, chunk),
        out_shape=jax.ShapeDtypeStruct((heads, cols, dim), f32),
        in_specs=[vmem, vmem, vmem, pl.BlockSpec(memory_space=pl.ANY), vmem, vmem, vmem, vmem],
        out_specs=vmem,
        scratch_shapes=[
            pltpu.VMEM((chips, heads, rows, lanes), bf16),
            pltpu.VMEM((chips - 1, heads, rows, lanes), bf16),
            pltpu.VMEM((chips - 1, heads, rows, lanes), bf16),
            pltpu.VMEM((tp - 1, blocks_dev, block), f32),
            pltpu.VMEM((peers, heads, cols, dim), bf16),
            pltpu.VMEM((peers, aux_rows, cols), f32),
            pltpu.VMEM((heads, rows, lanes), bf16),
            pltpu.VMEM((heads, pool, block, lanes), bf16),
            pltpu.VMEM((max(pool, blocks_dev) * block, cols), f32),
            pltpu.VMEM((dim, cols), f32),
            pltpu.VMEM((heads, dim, cols), f32),
            pltpu.VMEM((peers, heads, dim, cols), bf16),
            pltpu.VMEM((peers, heads, dim, cols), bf16),
            pltpu.VMEM((peers, heads, 8, cols), f32),
            pltpu.VMEM((peers, heads, 8, cols), f32),
            pltpu.VMEM((heads, dim, cols), f32),
            dma((chips, chunks)), dma((chips, chunks)),
            dma((chips - 1, chunks)), dma((chips - 1, chunks)),
            dma((tp - 1,)), dma((tp - 1,)),
            dma((peers,)), dma((peers,)),
            dma((peers,)), dma((peers,)),
            dma((peers,)), dma((peers,)),
            dma((peers,)), dma((peers,)),
            dma(()),
        ],
        compiler_params=pltpu.CompilerParams(
            collective_id=0, has_side_effects=True, vmem_limit_bytes=48 * 1024 * 1024
        ),
    )(
        part,
        squares,
        decode_query.reshape(heads, cols, dim),
        resident_cache,
        new_kv,
        full[:pool],
        edge[:pool],
        aux,
    )
    return out.reshape(heads, requests, group_size, dim)


def solution(mesh):
    sizes = dict(mesh.shape)
    return jax.shard_map(
        functools.partial(per_device, sizes["section"], sizes["tp"]),
        mesh=mesh,
        in_specs=(
            P(("groups", "section"), "tp"),
            P("tp"),
            P("tp", None, None),
            P("groups", None),
            P("tp", ("groups", "section"), None, None),
            P(("groups", "section"), None),
            P(("groups", "section")),
            P("tp", ("groups", "section"), None, None),
            P("tp", ("groups", "section"), None),
        ),
        out_specs=P("tp", ("groups", "section"), None, None),
        check_vma=False,
    )
```

```python
import functools
import math

import jax
import jax.numpy as jnp
from jax import lax
from jax.experimental import pallas as pl
from jax.experimental.pallas import tpu as pltpu
from jax.sharding import PartitionSpec as P

D = 8192


EPSILON = 1e-05
NEG = -1e30
GROUP = 4
MESH = pl.DeviceIdType.MESH


def count_pages(
    sections, heads, pool, block, owner_ref, table_ref, length_ref, full_ref, edge_ref, aux_ref
):
    total_blocks = owner_ref.shape[0]
    blocks_dev = total_blocks // sections
    slots_peer = 2 * ((blocks_dev + sections - 1) // sections)
    requests, depth = table_ref.shape
    cols = full_ref.shape[1]
    me = lax.axis_index("section")
    f32 = jnp.float32

    def iota(shape, axis):
        return lax.broadcasted_iota(jnp.int32, shape, axis)

    grid = (total_blocks, total_blocks)
    across = jnp.broadcast_to(owner_ref[...], grid)
    row, column = iota(grid, 0), iota(grid, 1)
    along = jnp.sum(jnp.where(row == column, across, 0).astype(f32), axis=0, keepdims=True)
    earlier = (across.astype(f32) == along) & (column < row)
    earlier = earlier & (lax.div(column, blocks_dev) == lax.div(row, blocks_dev))
    rank = jnp.sum(jnp.where(earlier, 1.0, 0.0), axis=1, keepdims=True)
    tall = (total_blocks, 1)
    slot = pool + lax.div(iota(tall, 0), blocks_dev) * slots_peer
    placed = jnp.where(owner_ref[...] == me, slot.astype(f32) + rank, -1.0)

    spread = iota((requests, cols), 0) == lax.div(iota((requests, cols), 1), cols // requests)
    spread = jnp.where(spread, 1.0, 0.0)
    contract = (((0,), (0,)), ((), ()))
    columns = lax.dot_general(
        table_ref[...].astype(f32), spread, contract, preferred_element_type=f32
    )
    length = jnp.broadcast_to(length_ref[...], (8, requests))
    split = lax.div(length, block)
    blocks_held = jnp.dot(split.astype(f32), spread, preferred_element_type=f32)[:1]
    rest = jnp.dot((length - split * block).astype(f32), spread, preferred_element_type=f32)[:1]

    def counts(pages):
        full = jnp.zeros((pages.shape[0], cols), f32)
        edge = jnp.zeros((pages.shape[0], cols), f32)
        for j in range(depth):
            same = jnp.where(pages == columns[j : j + 1], 1.0, 0.0)
            full = full + jnp.where(blocks_held > j, same, 0.0)
            edge = edge + jnp.where(blocks_held == j, same, 0.0)
        return full, edge

    full, edge = counts(iota((pool, 1), 0).astype(f32))
    full_ref[...] = full
    edge_ref[...] = edge
    zeros = (blocks_held * block + rest) - jnp.sum(full * block + edge * rest, axis=0, keepdims=True)
    full, edge = counts(placed)
    zeros = zeros - jnp.sum(full * block + edge * rest, axis=0, keepdims=True)
    for s in range(sections):
        at = slice(s * blocks_dev, (s + 1) * blocks_dev)
        aux_ref[s, :blocks_dev] = full[at]
        aux_ref[s, blocks_dev : 2 * blocks_dev] = edge[at]
        aux_ref[s, 2 * blocks_dev :] = jnp.concatenate(
            [rest, zeros, jnp.zeros((6, cols), f32)], axis=0
        )


def kernel(
    sections, tp, heads, block, chunk,
    part_ref, token_ref, query_ref, cache_ref, fresh_ref, owner_ref, table_ref, length_ref,
    out_ref,
    tokens, sq_ref, full_ref, edge_ref, aux_ref,
    sib, cross_out, cross_in, sq_in, query_in, aux_in, kv, pages, scores, acc, res_acc,
    back_out, back_in, stat_out, stat_in, own_acc,
    sib_s, sib_r, cross_s, cross_r, sq_s, sq_r, query_s, query_r, aux_s, aux_r,
    back_s, back_r, stat_s, stat_r, page_s, token_s,
):
    me = lax.axis_index("section")
    t = lax.axis_index("tp")
    core, x = lax.rem(t, 2), lax.div(t, 2)
    chips = tp // 2
    rows = part_ref.shape[1]
    chunks = rows // chunk
    cols = query_ref.shape[1]
    dim = query_ref.shape[2]
    pool = cache_ref.shape[1]
    blocks_dev = rows // block
    scale = 1.0 / math.sqrt(dim)

    barrier = pltpu.get_barrier_semaphore()
    for d in range(1, tp):
        pl.semaphore_signal(
            barrier, inc=1, device_id={"tp": lax.rem(t + d, tp)}, device_id_type=MESH
        )
    for d in range(1, sections):
        pl.semaphore_signal(
            barrier, inc=1, device_id={"section": lax.rem(me + d, sections)}, device_id_type=MESH
        )
    pl.semaphore_wait(barrier, tp + sections - 2)

    def span(i):
        return pl.ds(pl.multiple_of(i * chunk, chunk), chunk)

    def sib_copy(d, h, i):
        group = lax.rem(x + d, chips) * 2 + 1 - core
        return pltpu.make_async_remote_copy(
            src_ref=part_ref.at[group * heads + h, span(i)],
            dst_ref=sib.at[d, h, span(i)],
            send_sem=sib_s.at[d, h, i],
            recv_sem=sib_r.at[d, h, i],
            device_id={"tp": x * 2 + 1 - core},
            device_id_type=MESH,
        )

    def cross_copy(d, h, i):
        return pltpu.make_async_remote_copy(
            src_ref=cross_out.at[d - 1, h, span(i)],
            dst_ref=cross_in.at[d - 1, h, span(i)],
            send_sem=cross_s.at[d - 1, h, i],
            recv_sem=cross_r.at[d - 1, h, i],
            device_id={"tp": lax.rem(x + d, chips) * 2 + core},
            device_id_type=MESH,
        )

    def sq_copy(d):
        return pltpu.make_async_remote_copy(
            src_ref=sq_ref,
            dst_ref=sq_in.at[d - 1],
            send_sem=sq_s.at[d - 1],
            recv_sem=sq_r.at[d - 1],
            device_id={"tp": lax.rem(t + d, tp)},
            device_id_type=MESH,
        )

    def query_copy(d):
        return pltpu.make_async_remote_copy(
            src_ref=query_ref,
            dst_ref=query_in.at[d - 1],
            send_sem=query_s.at[d - 1],
            recv_sem=query_r.at[d - 1],
            device_id={"section": lax.rem(me + d, sections)},
            device_id_type=MESH,
        )

    def aux_copy(d):
        peer = lax.rem(me + d, sections)
        return pltpu.make_async_remote_copy(
            src_ref=aux_ref.at[peer],
            dst_ref=aux_in.at[d - 1],
            send_sem=aux_s.at[d - 1],
            recv_sem=aux_r.at[d - 1],
            device_id={"section": peer},
            device_id_type=MESH,
        )

    def back_copy(d, h):
        return pltpu.make_async_remote_copy(
            src_ref=back_out.at[d - 1, h],
            dst_ref=back_in.at[d - 1, h],
            send_sem=back_s.at[d - 1, h],
            recv_sem=back_r.at[d - 1, h],
            device_id={"section": lax.rem(me + sections - d, sections)},
            device_id_type=MESH,
        )

    def stat_copy(d, h):
        return pltpu.make_async_remote_copy(
            src_ref=stat_out.at[d - 1, h],
            dst_ref=stat_in.at[d - 1, h],
            send_sem=stat_s.at[d - 1, h],
            recv_sem=stat_r.at[d - 1, h],
            device_id={"section": lax.rem(me + sections - d, sections)},
            device_id_type=MESH,
        )

    def page_copy():
        return pltpu.make_async_copy(cache_ref, pages, page_s)

    def token_copy():
        return pltpu.make_async_copy(token_ref, tokens, token_s)

    for h in range(heads):
        for d in range(1, chips):
            for i in range(chunks):
                sib_copy(d, h, i).start()
    token_copy().start()
    page_copy().start()
    for d in range(1, sections):
        query_copy(d).start()

    count_pages(
        sections, heads, pool, block, owner_ref, table_ref, length_ref, full_ref, edge_ref, aux_ref
    )
    for d in range(1, sections):
        aux_copy(d).start()

    def cross(h):
        for d in range(1, chips):
            group = lax.rem(x + d, chips) * 2 + core
            for i in range(chunks):
                sib_copy(d, h, i).wait_recv()
                mine = part_ref[group * heads + h, span(i)]
                theirs = sib[d, h, span(i)]
                cross_out[d - 1, h, span(i)] = (
                    mine.astype(jnp.float32) + theirs.astype(jnp.float32)
                ).astype(jnp.bfloat16)
                if h == 0:
                    cross_copy(d, h, i).start()

    for h in range(heads):
        cross(h)
    for h in range(heads):
        for i in range(chunks):
            sib_copy(0, h, i).start()

    token_copy().wait()

    def square(j, carry):
        total = jnp.zeros((block, 128), jnp.float32)
        at = pl.ds(pl.multiple_of(j * block, block), block)
        for k in range(tokens.shape[1] // 128):
            piece = tokens[at, k * 128 : (k + 1) * 128].astype(jnp.float32)
            total = total + piece * piece
        sq_ref[pl.ds(j, 1), :] = jnp.sum(jnp.transpose(total), axis=0, keepdims=True)
        return carry

    lax.fori_loop(0, blocks_dev, square, 0)
    for d in range(1, tp):
        sq_copy(d).start()

    position = lax.broadcasted_iota(jnp.int32, (block, cols), 0).astype(jnp.float32)

    def attend(query, load, count_rows, rest, n_pages, extra=None, zeros=None):
        inside = position < rest

        def count(p):
            full, edge = count_rows(p)
            return full + jnp.where(inside, edge, 0.0)

        def first(step, top):
            base = step * GROUP
            for k in range(GROUP):
                keys = load(base + k)[:, :dim]
                s = lax.dot_general(
                    keys, query, (((1,), (1,)), ((), ())), preferred_element_type=jnp.float32
                ) * scale
                s = jnp.where(count(base + k) > 0, s, NEG)
                scores[pl.ds(pl.multiple_of((base + k) * block, block), block)] = s
                top = jnp.maximum(top, jnp.max(s.reshape(block // 8, 8, cols), axis=0))
            return top

        top = lax.fori_loop(0, n_pages // GROUP, first, jnp.full((8, cols), NEG, jnp.float32))
        top = jnp.max(top, axis=0, keepdims=True)
        if extra is not None:
            fresh = extra
            requests = fresh.shape[0]
            own = (
                lax.broadcasted_iota(jnp.int32, (requests, cols), 0) * (cols // requests)
            )
            column = lax.broadcasted_iota(jnp.int32, (requests, cols), 1)
            own = (column >= own) & (column < own + cols // requests)
            s_own = lax.dot_general(
                fresh[:, :dim], query, (((1,), (1,)), ((), ())), preferred_element_type=jnp.float32
            ) * scale
            s_own = jnp.where(own, s_own, NEG)
            top = jnp.maximum(top, jnp.max(s_own, axis=0, keepdims=True))
            top = jnp.maximum(top, jnp.where(zeros > 0, 0.0, NEG))
            w_own = jnp.where(own, jnp.exp(s_own - top), 0.0)
            acc[...] = lax.dot_general(
                fresh[:, dim:], w_own.astype(jnp.bfloat16), (((0,), (0,)), ((), ())),
                preferred_element_type=jnp.float32,
            )
            total = jnp.sum(w_own, axis=0, keepdims=True)
            total = total + jnp.where(zeros > 0, zeros * jnp.exp(0.0 - top), 0.0)
        else:
            acc[...] = jnp.zeros_like(acc)
            total = jnp.zeros((1, cols), jnp.float32)

        def second(step, total8):
            base = step * GROUP
            values, lows = [], []
            for k in range(GROUP):
                s = scores[pl.ds(pl.multiple_of((base + k) * block, block), block)]
                w = jnp.exp(s - top)
                c = count(base + k)
                total8 = total8 + jnp.sum((w * c).reshape(block // 8, 8, cols), axis=0)
                low = w.astype(jnp.bfloat16).astype(jnp.float32) * c
                lows.append(low.astype(jnp.bfloat16))
                values.append(load(base + k)[:, dim:])
            acc[...] += lax.dot_general(
                jnp.concatenate(values, axis=0), jnp.concatenate(lows, axis=0),
                (((0,), (0,)), ((), ())), preferred_element_type=jnp.float32,
            )
            return total8

        total8 = lax.fori_loop(0, n_pages // GROUP, second, jnp.zeros((8, cols), jnp.float32))
        return top, total + jnp.sum(total8, axis=0, keepdims=True)

    page_copy().wait()
    rest_own = aux_ref[0, 2 * blocks_dev : 2 * blocks_dev + 1, :]
    zeros_own = aux_ref[0, 2 * blocks_dev + 1 : 2 * blocks_dev + 2, :]
    res_stats = []
    for h in range(heads):
        stat = attend(
            query_ref[h],
            lambda p, h=h: pages[h, p],
            lambda p: (full_ref[pl.ds(p, 1), :], edge_ref[pl.ds(p, 1), :]),
            rest_own,
            pool,
            fresh_ref[h],
            zeros_own,
        )
        res_stats.append(stat)
        res_acc[h] = acc[...]

    for d in range(1, tp):
        sq_copy(d).wait_recv()
    squares = sq_ref[...]
    for d in range(1, tp):
        squares = squares + sq_in[d - 1]
    inverse = lax.rsqrt(squares / D + EPSILON)
    diagonal = lax.broadcasted_iota(jnp.int32, (block, block), 0) == lax.broadcasted_iota(
        jnp.int32, (block, block), 1
    )
    per_chunk = chunk // block

    def load_block(h):
        return lambda p: kv[h, pl.ds(pl.multiple_of(p * block, block), block)]

    for h in range(heads):
        if h + 1 < heads:
            for d in range(1, chips):
                for i in range(chunks):
                    cross_copy(d, h, i).wait_send()
            for d in range(1, chips):
                for i in range(chunks):
                    cross_copy(d, h + 1, i).start()
        for i in range(chunks):
            sib_copy(0, h, i).wait_recv()
            for d in range(1, chips):
                cross_copy(d, h, i).wait_recv()
            for k in range(per_chunk):
                j = i * per_chunk + k
                lanes = inverse[j : j + 1, :]
                factor = jnp.sum(
                    jnp.where(diagonal, jnp.broadcast_to(lanes, (block, block)), 0.0),
                    axis=1,
                    keepdims=True,
                )
                at = slice(j * block, (j + 1) * block)
                value = part_ref[t * heads + h, at].astype(jnp.float32) + sib[0, h, at].astype(
                    jnp.float32
                )
                for d in range(1, chips):
                    value = value + cross_in[d - 1, h, at].astype(jnp.float32)
                kv[h, at] = (value * factor).astype(jnp.bfloat16)

        def serve(d, carry, h=h):
            if h == 0:
                query_copy(d).wait_recv()
                aux_copy(d).wait_recv()
            top, total = attend(
                query_in[d - 1, h],
                load_block(h),
                lambda p: (
                    aux_in[d - 1, pl.ds(p, 1), :],
                    aux_in[d - 1, pl.ds(blocks_dev + p, 1), :],
                ),
                aux_in[d - 1, 2 * blocks_dev : 2 * blocks_dev + 1, :],
                blocks_dev,
            )
            back_out[d - 1, h] = acc[...].astype(jnp.bfloat16)
            stat_out[d - 1, h] = jnp.concatenate(
                [top, total, jnp.zeros((6, cols), jnp.float32)], axis=0
            )
            back_copy(d, h).start()
            stat_copy(d, h).start()
            return carry

        lax.fori_loop(1, sections, serve, 0)

    own_stats = []
    for h in range(heads):
        stat = attend(
            query_ref[h],
            load_block(h),
            lambda p: (
                aux_ref[me, pl.ds(p, 1), :],
                aux_ref[me, pl.ds(blocks_dev + p, 1), :],
            ),
            rest_own,
            blocks_dev,
        )
        own_stats.append(stat)
        own_acc[h] = acc[...]

    for h in range(heads):
        for d in range(1, sections):
            back_copy(d, h).wait_recv()
            stat_copy(d, h).wait_recv()
        tops = [res_stats[h][0], own_stats[h][0]]
        totals = [res_stats[h][1], own_stats[h][1]]
        for d in range(1, sections):
            tops.append(stat_in[d - 1, h, 0:1, :])
            totals.append(stat_in[d - 1, h, 1:2, :])
        top = functools.reduce(jnp.maximum, tops)
        factors = [jnp.exp(one - top) for one in tops]
        total = sum(f * one for f, one in zip(factors, totals))
        mixed = res_acc[h] * factors[0] + own_acc[h] * factors[1]
        for d in range(1, sections):
            mixed = mixed + back_in[d - 1, h].astype(jnp.float32) * factors[d + 1]
        out_ref[h] = jnp.transpose(mixed / total)

    for h in range(heads):
        for i in range(chunks):
            for d in range(chips):
                sib_copy(d, h, i).wait_send()
                if d and h == heads - 1:
                    cross_copy(d, h, i).wait_send()
    for d in range(1, tp):
        sq_copy(d).wait_send()
    for d in range(1, sections):
        query_copy(d).wait_send()
        aux_copy(d).wait_send()
        for h in range(heads):
            back_copy(d, h).wait_send()
            stat_copy(d, h).wait_send()


def per_device(
    sections,
    tp,
    tokens,
    norm_gain,
    kv_weight,
    block_owner,
    resident_cache,
    page_table,
    context_len,
    decode_query,
    new_kv,
):
    heads, pool, block, lanes = resident_cache.shape
    _, requests, group_size, dim = decode_query.shape
    cols = requests * group_size
    rows = tokens.shape[0]
    blocks_dev = rows // block
    chunk = min(rows, 512)
    chunks = rows // chunk
    chips = tp // 2
    widened = tokens.astype(jnp.float32)
    normed = (widened * norm_gain.astype(jnp.float32)[None, :]).astype(jnp.bfloat16)
    part = jnp.einsum(
        "td,dhc->htc", normed, kv_weight, preferred_element_type=jnp.float32
    ).astype(jnp.bfloat16)
    aux_rows = 2 * blocks_dev + 8
    vmem = pl.BlockSpec(memory_space=pltpu.VMEM)
    anywhere = pl.BlockSpec(memory_space=pl.ANY)
    dma = pltpu.SemaphoreType.DMA
    peers = sections - 1
    bf16, f32 = jnp.bfloat16, jnp.float32
    out = pl.pallas_call(
        functools.partial(kernel, sections, tp, heads, block, chunk),
        out_shape=jax.ShapeDtypeStruct((heads, cols, dim), f32),
        in_specs=[vmem, anywhere, vmem, anywhere, vmem, vmem, vmem, vmem],
        out_specs=vmem,
        scratch_shapes=[
            pltpu.VMEM(tokens.shape, bf16),
            pltpu.VMEM((blocks_dev, block), f32),
            pltpu.VMEM((pool, cols), f32),
            pltpu.VMEM((pool, cols), f32),
            pltpu.VMEM((sections, aux_rows, cols), f32),
            pltpu.VMEM((chips, heads, rows, lanes), bf16),
            pltpu.VMEM((chips - 1, heads, rows, lanes), bf16),
            pltpu.VMEM((chips - 1, heads, rows, lanes), bf16),
            pltpu.VMEM((tp - 1, blocks_dev, block), f32),
            pltpu.VMEM((peers, heads, cols, dim), bf16),
            pltpu.VMEM((peers, aux_rows, cols), f32),
            pltpu.VMEM((heads, rows, lanes), bf16),
            pltpu.VMEM((heads, pool, block, lanes), bf16),
            pltpu.VMEM((max(pool, blocks_dev) * block, cols), f32),
            pltpu.VMEM((dim, cols), f32),
            pltpu.VMEM((heads, dim, cols), f32),
            pltpu.VMEM((peers, heads, dim, cols), bf16),
            pltpu.VMEM((peers, heads, dim, cols), bf16),
            pltpu.VMEM((peers, heads, 8, cols), f32),
            pltpu.VMEM((peers, heads, 8, cols), f32),
            pltpu.VMEM((heads, dim, cols), f32),
            dma((chips, heads, chunks)), dma((chips, heads, chunks)),
            dma((chips - 1, heads, chunks)), dma((chips - 1, heads, chunks)),
            dma((tp - 1,)), dma((tp - 1,)),
            dma((peers,)), dma((peers,)),
            dma((peers,)), dma((peers,)),
            dma((peers, heads)), dma((peers, heads)),
            dma((peers, heads)), dma((peers, heads)),
            dma(()),
            dma(()),
        ],
        compiler_params=pltpu.CompilerParams(
            collective_id=0, has_side_effects=True, vmem_limit_bytes=48 * 1024 * 1024
        ),
    )(
        part,
        tokens,
        decode_query.reshape(heads, cols, dim),
        resident_cache,
        new_kv,
        block_owner,
        page_table,
        context_len.reshape(1, requests),
    )
    return out.reshape(heads, requests, group_size, dim)


def solution(mesh):
    sizes = dict(mesh.shape)
    return jax.shard_map(
        functools.partial(per_device, sizes["section"], sizes["tp"]),
        mesh=mesh,
        in_specs=(
            P(("groups", "section"), "tp"),
            P("tp"),
            P("tp", None, None),
            P("groups", None),
            P("tp", ("groups", "section"), None, None),
            P(("groups", "section"), None),
            P(("groups", "section")),
            P("tp", ("groups", "section"), None, None),
            P("tp", ("groups", "section"), None),
        ),
        out_specs=P("tp", ("groups", "section"), None, None),
        check_vma=False,
    )
```

```python
import functools
import math

import jax
import jax.numpy as jnp
from jax import lax
from jax.experimental import pallas as pl
from jax.experimental.pallas import tpu as pltpu
from jax.sharding import PartitionSpec as P

D = 8192


EPSILON = 1e-05
NEG = -1e30
GROUP = 4
MESH = pl.DeviceIdType.MESH


def count_pages(
    sections, heads, pool, block, owner_ref, table_ref, length_ref, full_ref, edge_ref, aux_ref
):
    total_blocks = owner_ref.shape[0]
    blocks_dev = total_blocks // sections
    slots_peer = 2 * ((blocks_dev + sections - 1) // sections)
    requests, depth = table_ref.shape
    cols = full_ref.shape[1]
    me = lax.axis_index("section")
    f32 = jnp.float32

    def iota(shape, axis):
        return lax.broadcasted_iota(jnp.int32, shape, axis)

    grid = (total_blocks, total_blocks)
    across = jnp.broadcast_to(owner_ref[...], grid)
    row, column = iota(grid, 0), iota(grid, 1)
    along = jnp.sum(jnp.where(row == column, across, 0).astype(f32), axis=0, keepdims=True)
    earlier = (across.astype(f32) == along) & (column < row)
    earlier = earlier & (lax.div(column, blocks_dev) == lax.div(row, blocks_dev))
    rank = jnp.sum(jnp.where(earlier, 1.0, 0.0), axis=1, keepdims=True)
    tall = (total_blocks, 1)
    slot = pool + lax.div(iota(tall, 0), blocks_dev) * slots_peer
    placed = jnp.where(owner_ref[...] == me, slot.astype(f32) + rank, -1.0)

    spread = iota((requests, cols), 0) == lax.div(iota((requests, cols), 1), cols // requests)
    spread = jnp.where(spread, 1.0, 0.0)
    contract = (((0,), (0,)), ((), ()))
    columns = lax.dot_general(
        table_ref[...].astype(f32), spread, contract, preferred_element_type=f32
    )
    length = jnp.broadcast_to(length_ref[...], (8, requests))
    split = lax.div(length, block)
    blocks_held = jnp.dot(split.astype(f32), spread, preferred_element_type=f32)[:1]
    rest = jnp.dot((length - split * block).astype(f32), spread, preferred_element_type=f32)[:1]

    def counts(pages):
        full = jnp.zeros((pages.shape[0], cols), f32)
        edge = jnp.zeros((pages.shape[0], cols), f32)
        for j in range(depth):
            same = jnp.where(pages == columns[j : j + 1], 1.0, 0.0)
            full = full + jnp.where(blocks_held > j, same, 0.0)
            edge = edge + jnp.where(blocks_held == j, same, 0.0)
        return full, edge

    full, edge = counts(iota((pool, 1), 0).astype(f32))
    full_ref[...] = full
    edge_ref[...] = edge
    zeros = (blocks_held * block + rest) - jnp.sum(full * block + edge * rest, axis=0, keepdims=True)
    full, edge = counts(placed)
    zeros = zeros - jnp.sum(full * block + edge * rest, axis=0, keepdims=True)
    for s in range(sections):
        at = slice(s * blocks_dev, (s + 1) * blocks_dev)
        aux_ref[s, :blocks_dev] = full[at]
        aux_ref[s, blocks_dev : 2 * blocks_dev] = edge[at]
        aux_ref[s, 2 * blocks_dev :] = jnp.concatenate(
            [rest, zeros, jnp.zeros((6, cols), f32)], axis=0
        )


def kernel(
    sections, tp, heads, block, chunk,
    token_ref, gain_ref, weight_ref, query_ref, cache_ref, fresh_ref, owner_ref, table_ref, length_ref,
    out_ref,
    tokens, raw, weights, part_ref, sq_ref, full_ref, edge_ref, aux_ref,
    sib, cross_out, cross_in, sq_in, query_in, aux_in, kv, pages, scores, acc, res_acc,
    back_out, back_in, stat_out, stat_in, own_acc,
    sib_s, sib_r, cross_s, cross_r, sq_s, sq_r, query_s, query_r, aux_s, aux_r,
    back_s, back_r, stat_s, stat_r, page_s, token_s, raw_s,
):
    me = lax.axis_index("section")
    t = lax.axis_index("tp")
    core, x = lax.rem(t, 2), lax.div(t, 2)
    chips = tp // 2
    rows = part_ref.shape[1]
    chunks = rows // chunk
    cols = query_ref.shape[1]
    dim = query_ref.shape[2]
    pool = cache_ref.shape[1]
    blocks_dev = rows // block
    scale = 1.0 / math.sqrt(dim)

    barrier = pltpu.get_barrier_semaphore()
    for d in range(1, tp):
        pl.semaphore_signal(
            barrier, inc=1, device_id={"tp": lax.rem(t + d, tp)}, device_id_type=MESH
        )
    for d in range(1, sections):
        pl.semaphore_signal(
            barrier, inc=1, device_id={"section": lax.rem(me + d, sections)}, device_id_type=MESH
        )
    pl.semaphore_wait(barrier, tp + sections - 2)

    def span(i):
        return pl.ds(pl.multiple_of(i * chunk, chunk), chunk)

    def sib_copy(d, h, i):
        group = lax.rem(x + d, chips) * 2 + 1 - core
        return pltpu.make_async_remote_copy(
            src_ref=part_ref.at[group * heads + h, span(i)],
            dst_ref=sib.at[d, h, span(i)],
            send_sem=sib_s.at[d, h, i],
            recv_sem=sib_r.at[d, h, i],
            device_id={"tp": x * 2 + 1 - core},
            device_id_type=MESH,
        )

    def cross_copy(d, h, i):
        return pltpu.make_async_remote_copy(
            src_ref=cross_out.at[d - 1, h, span(i)],
            dst_ref=cross_in.at[d - 1, h, span(i)],
            send_sem=cross_s.at[d - 1, h, i],
            recv_sem=cross_r.at[d - 1, h, i],
            device_id={"tp": lax.rem(x + d, chips) * 2 + core},
            device_id_type=MESH,
        )

    def sq_copy(d):
        return pltpu.make_async_remote_copy(
            src_ref=sq_ref,
            dst_ref=sq_in.at[d - 1],
            send_sem=sq_s.at[d - 1],
            recv_sem=sq_r.at[d - 1],
            device_id={"tp": lax.rem(t + d, tp)},
            device_id_type=MESH,
        )

    def query_copy(d):
        return pltpu.make_async_remote_copy(
            src_ref=query_ref,
            dst_ref=query_in.at[d - 1],
            send_sem=query_s.at[d - 1],
            recv_sem=query_r.at[d - 1],
            device_id={"section": lax.rem(me + d, sections)},
            device_id_type=MESH,
        )

    def aux_copy(d):
        peer = lax.rem(me + d, sections)
        return pltpu.make_async_remote_copy(
            src_ref=aux_ref.at[peer],
            dst_ref=aux_in.at[d - 1],
            send_sem=aux_s.at[d - 1],
            recv_sem=aux_r.at[d - 1],
            device_id={"section": peer},
            device_id_type=MESH,
        )

    def back_copy(d, h):
        return pltpu.make_async_remote_copy(
            src_ref=back_out.at[d - 1, h],
            dst_ref=back_in.at[d - 1, h],
            send_sem=back_s.at[d - 1, h],
            recv_sem=back_r.at[d - 1, h],
            device_id={"section": lax.rem(me + sections - d, sections)},
            device_id_type=MESH,
        )

    def stat_copy(d, h):
        return pltpu.make_async_remote_copy(
            src_ref=stat_out.at[d - 1, h],
            dst_ref=stat_in.at[d - 1, h],
            send_sem=stat_s.at[d - 1, h],
            recv_sem=stat_r.at[d - 1, h],
            device_id={"section": lax.rem(me + sections - d, sections)},
            device_id_type=MESH,
        )

    def page_copy():
        return pltpu.make_async_copy(cache_ref, pages, page_s)

    raw_rows = raw.shape[0] // blocks_dev

    def token_copy(j):
        at = pl.ds(pl.multiple_of(j * block, block), block)
        return pltpu.make_async_copy(token_ref.at[at], tokens.at[at], token_s.at[j])

    def raw_copy(j):
        at = pl.ds(pl.multiple_of(j * raw_rows, raw_rows), raw_rows)
        return pltpu.make_async_copy(weight_ref.at[at], raw.at[at], raw_s.at[j])

    for j in range(blocks_dev):
        raw_copy(j).start()
        token_copy(j).start()
    page_copy().start()
    for d in range(1, sections):
        query_copy(d).start()

    count_pages(
        sections, heads, pool, block, owner_ref, table_ref, length_ref, full_ref, edge_ref, aux_ref
    )
    for d in range(1, sections):
        aux_copy(d).start()

    all_heads = weights.shape[0]
    tile = 256
    deep = tile // all_heads
    to, at_row = lax.broadcasted_iota(jnp.int32, (tile, tile), 0), lax.broadcasted_iota(
        jnp.int32, (tile, tile), 1
    )
    order = jnp.where(
        at_row == lax.rem(to, deep) * all_heads + lax.div(to, deep), 1.0, 0.0
    ).astype(jnp.bfloat16)

    def prepare(j, carry):
        raw_copy(j).wait()
        token_copy(j).wait()
        total = jnp.zeros((block, 128), jnp.float32)
        at = pl.ds(pl.multiple_of(j * block, block), block)
        for k in range(tokens.shape[1] // 128):
            lanes = slice(k * 128, (k + 1) * 128)
            piece = tokens[at, lanes].astype(jnp.float32)
            total = total + piece * piece
            tokens[at, lanes] = (piece * gain_ref[:, lanes]).astype(jnp.bfloat16)
        sq_ref[pl.ds(j, 1), :] = jnp.sum(jnp.transpose(total), axis=0, keepdims=True)
        for k in range(raw_rows // tile):
            first = pl.multiple_of(j * raw_rows + k * tile, tile)
            rows_k = jnp.dot(
                order, raw[pl.ds(first, tile)], preferred_element_type=jnp.float32
            ).astype(jnp.bfloat16)
            depth = pl.multiple_of(j * (raw_rows // all_heads) + k * deep, deep)
            weights[:, pl.ds(depth, deep)] = rows_k.reshape(all_heads, deep, raw.shape[1])
        return carry

    lax.fori_loop(0, blocks_dev, prepare, 0)
    for d in range(1, tp):
        sq_copy(d).start()

    def project(head, send):
        for i in range(chunks):
            part_ref[head, span(i)] = jnp.dot(
                tokens[span(i), :], weights[head], preferred_element_type=jnp.float32
            ).astype(jnp.bfloat16)
            if send is not None:
                sib_copy(send[0], send[1], i).start()

    def cross(h):
        for d in range(1, chips):
            group = lax.rem(x + d, chips) * 2 + core
            for i in range(chunks):
                sib_copy(d, h, i).wait_recv()
                mine = part_ref[group * heads + h, span(i)]
                theirs = sib[d, h, span(i)]
                cross_out[d - 1, h, span(i)] = (
                    mine.astype(jnp.float32) + theirs.astype(jnp.float32)
                ).astype(jnp.bfloat16)
                if h == 0:
                    cross_copy(d, h, i).start()

    for h in range(heads):
        for d in range(1, chips):
            project((lax.rem(x + d, chips) * 2 + 1 - core) * heads + h, (d, h))
        for d in range(1, chips):
            project((lax.rem(x + d, chips) * 2 + core) * heads + h, None)
        cross(h)
    for h in range(heads):
        project((x * 2 + 1 - core) * heads + h, (0, h))
    for h in range(heads):
        project(t * heads + h, None)

    position = lax.broadcasted_iota(jnp.int32, (block, cols), 0).astype(jnp.float32)

    def attend(query, load, count_rows, rest, n_pages, extra=None, zeros=None):
        inside = position < rest

        def count(p):
            full, edge = count_rows(p)
            return full + jnp.where(inside, edge, 0.0)

        def first(step, top):
            base = step * GROUP
            for k in range(GROUP):
                keys = load(base + k)[:, :dim]
                s = lax.dot_general(
                    keys, query, (((1,), (1,)), ((), ())), preferred_element_type=jnp.float32
                ) * scale
                s = jnp.where(count(base + k) > 0, s, NEG)
                scores[pl.ds(pl.multiple_of((base + k) * block, block), block)] = s
                top = jnp.maximum(top, jnp.max(s.reshape(block // 8, 8, cols), axis=0))
            return top

        top = lax.fori_loop(0, n_pages // GROUP, first, jnp.full((8, cols), NEG, jnp.float32))
        top = jnp.max(top, axis=0, keepdims=True)
        if extra is not None:
            fresh = extra
            requests = fresh.shape[0]
            own = (
                lax.broadcasted_iota(jnp.int32, (requests, cols), 0) * (cols // requests)
            )
            column = lax.broadcasted_iota(jnp.int32, (requests, cols), 1)
            own = (column >= own) & (column < own + cols // requests)
            s_own = lax.dot_general(
                fresh[:, :dim], query, (((1,), (1,)), ((), ())), preferred_element_type=jnp.float32
            ) * scale
            s_own = jnp.where(own, s_own, NEG)
            top = jnp.maximum(top, jnp.max(s_own, axis=0, keepdims=True))
            top = jnp.maximum(top, jnp.where(zeros > 0, 0.0, NEG))
            w_own = jnp.where(own, jnp.exp(s_own - top), 0.0)
            acc[...] = lax.dot_general(
                fresh[:, dim:], w_own.astype(jnp.bfloat16), (((0,), (0,)), ((), ())),
                preferred_element_type=jnp.float32,
            )
            total = jnp.sum(w_own, axis=0, keepdims=True)
            total = total + jnp.where(zeros > 0, zeros * jnp.exp(0.0 - top), 0.0)
        else:
            acc[...] = jnp.zeros_like(acc)
            total = jnp.zeros((1, cols), jnp.float32)

        def second(step, total8):
            base = step * GROUP
            values, lows = [], []
            for k in range(GROUP):
                s = scores[pl.ds(pl.multiple_of((base + k) * block, block), block)]
                w = jnp.exp(s - top)
                c = count(base + k)
                total8 = total8 + jnp.sum((w * c).reshape(block // 8, 8, cols), axis=0)
                low = w.astype(jnp.bfloat16).astype(jnp.float32) * c
                lows.append(low.astype(jnp.bfloat16))
                values.append(load(base + k)[:, dim:])
            acc[...] += lax.dot_general(
                jnp.concatenate(values, axis=0), jnp.concatenate(lows, axis=0),
                (((0,), (0,)), ((), ())), preferred_element_type=jnp.float32,
            )
            return total8

        total8 = lax.fori_loop(0, n_pages // GROUP, second, jnp.zeros((8, cols), jnp.float32))
        return top, total + jnp.sum(total8, axis=0, keepdims=True)

    page_copy().wait()
    rest_own = aux_ref[0, 2 * blocks_dev : 2 * blocks_dev + 1, :]
    zeros_own = aux_ref[0, 2 * blocks_dev + 1 : 2 * blocks_dev + 2, :]
    res_stats = []
    for h in range(heads):
        stat = attend(
            query_ref[h],
            lambda p, h=h: pages[h, p],
            lambda p: (full_ref[pl.ds(p, 1), :], edge_ref[pl.ds(p, 1), :]),
            rest_own,
            pool,
            fresh_ref[h],
            zeros_own,
        )
        res_stats.append(stat)
        res_acc[h] = acc[...]

    for d in range(1, tp):
        sq_copy(d).wait_recv()
    squares = sq_ref[...]
    for d in range(1, tp):
        squares = squares + sq_in[d - 1]
    inverse = lax.rsqrt(squares / D + EPSILON)
    diagonal = lax.broadcasted_iota(jnp.int32, (block, block), 0) == lax.broadcasted_iota(
        jnp.int32, (block, block), 1
    )
    per_chunk = chunk // block

    def load_block(h):
        return lambda p: kv[h, pl.ds(pl.multiple_of(p * block, block), block)]

    for h in range(heads):
        if h + 1 < heads:
            for d in range(1, chips):
                for i in range(chunks):
                    cross_copy(d, h, i).wait_send()
            for d in range(1, chips):
                for i in range(chunks):
                    cross_copy(d, h + 1, i).start()
        for i in range(chunks):
            sib_copy(0, h, i).wait_recv()
            for d in range(1, chips):
                cross_copy(d, h, i).wait_recv()
            for k in range(per_chunk):
                j = i * per_chunk + k
                lanes = inverse[j : j + 1, :]
                factor = jnp.sum(
                    jnp.where(diagonal, jnp.broadcast_to(lanes, (block, block)), 0.0),
                    axis=1,
                    keepdims=True,
                )
                at = slice(j * block, (j + 1) * block)
                value = part_ref[t * heads + h, at].astype(jnp.float32) + sib[0, h, at].astype(
                    jnp.float32
                )
                for d in range(1, chips):
                    value = value + cross_in[d - 1, h, at].astype(jnp.float32)
                kv[h, at] = (value * factor).astype(jnp.bfloat16)

        def serve(d, carry, h=h):
            if h == 0:
                query_copy(d).wait_recv()
                aux_copy(d).wait_recv()
            top, total = attend(
                query_in[d - 1, h],
                load_block(h),
                lambda p: (
                    aux_in[d - 1, pl.ds(p, 1), :],
                    aux_in[d - 1, pl.ds(blocks_dev + p, 1), :],
                ),
                aux_in[d - 1, 2 * blocks_dev : 2 * blocks_dev + 1, :],
                blocks_dev,
            )
            back_out[d - 1, h] = acc[...].astype(jnp.bfloat16)
            stat_out[d - 1, h] = jnp.concatenate(
                [top, total, jnp.zeros((6, cols), jnp.float32)], axis=0
            )
            back_copy(d, h).start()
            stat_copy(d, h).start()
            return carry

        lax.fori_loop(1, sections, serve, 0)

    own_stats = []
    for h in range(heads):
        stat = attend(
            query_ref[h],
            load_block(h),
            lambda p: (
                aux_ref[me, pl.ds(p, 1), :],
                aux_ref[me, pl.ds(blocks_dev + p, 1), :],
            ),
            rest_own,
            blocks_dev,
        )
        own_stats.append(stat)
        own_acc[h] = acc[...]

    for h in range(heads):
        for d in range(1, sections):
            back_copy(d, h).wait_recv()
            stat_copy(d, h).wait_recv()
        tops = [res_stats[h][0], own_stats[h][0]]
        totals = [res_stats[h][1], own_stats[h][1]]
        for d in range(1, sections):
            tops.append(stat_in[d - 1, h, 0:1, :])
            totals.append(stat_in[d - 1, h, 1:2, :])
        top = functools.reduce(jnp.maximum, tops)
        factors = [jnp.exp(one - top) for one in tops]
        total = sum(f * one for f, one in zip(factors, totals))
        mixed = res_acc[h] * factors[0] + own_acc[h] * factors[1]
        for d in range(1, sections):
            mixed = mixed + back_in[d - 1, h].astype(jnp.float32) * factors[d + 1]
        out_ref[h] = jnp.transpose(mixed / total)

    for h in range(heads):
        for i in range(chunks):
            for d in range(chips):
                sib_copy(d, h, i).wait_send()
                if d and h == heads - 1:
                    cross_copy(d, h, i).wait_send()
    for d in range(1, tp):
        sq_copy(d).wait_send()
    for d in range(1, sections):
        query_copy(d).wait_send()
        aux_copy(d).wait_send()
        for h in range(heads):
            back_copy(d, h).wait_send()
            stat_copy(d, h).wait_send()


def per_device(
    sections,
    tp,
    tokens,
    norm_gain,
    kv_weight,
    block_owner,
    resident_cache,
    page_table,
    context_len,
    decode_query,
    new_kv,
):
    heads, pool, block, lanes = resident_cache.shape
    _, requests, group_size, dim = decode_query.shape
    cols = requests * group_size
    rows = tokens.shape[0]
    blocks_dev = rows // block
    chunk = min(rows, 512)
    chunks = rows // chunk
    chips = tp // 2
    features, all_heads, _ = kv_weight.shape
    aux_rows = 2 * blocks_dev + 8
    vmem = pl.BlockSpec(memory_space=pltpu.VMEM)
    anywhere = pl.BlockSpec(memory_space=pl.ANY)
    dma = pltpu.SemaphoreType.DMA
    peers = sections - 1
    bf16, f32 = jnp.bfloat16, jnp.float32
    out = pl.pallas_call(
        functools.partial(kernel, sections, tp, heads, block, chunk),
        out_shape=jax.ShapeDtypeStruct((heads, cols, dim), f32),
        in_specs=[anywhere, vmem, anywhere, vmem, anywhere, vmem, vmem, vmem, vmem],
        out_specs=vmem,
        scratch_shapes=[
            pltpu.VMEM(tokens.shape, bf16),
            pltpu.VMEM((features * all_heads, lanes), bf16),
            pltpu.VMEM((all_heads, features, lanes), bf16),
            pltpu.VMEM((all_heads, rows, lanes), bf16),
            pltpu.VMEM((blocks_dev, block), f32),
            pltpu.VMEM((pool, cols), f32),
            pltpu.VMEM((pool, cols), f32),
            pltpu.VMEM((sections, aux_rows, cols), f32),
            pltpu.VMEM((chips, heads, rows, lanes), bf16),
            pltpu.VMEM((chips - 1, heads, rows, lanes), bf16),
            pltpu.VMEM((chips - 1, heads, rows, lanes), bf16),
            pltpu.VMEM((tp - 1, blocks_dev, block), f32),
            pltpu.VMEM((peers, heads, cols, dim), bf16),
            pltpu.VMEM((peers, aux_rows, cols), f32),
            pltpu.VMEM((heads, rows, lanes), bf16),
            pltpu.VMEM((heads, pool, block, lanes), bf16),
            pltpu.VMEM((max(pool, blocks_dev) * block, cols), f32),
            pltpu.VMEM((dim, cols), f32),
            pltpu.VMEM((heads, dim, cols), f32),
            pltpu.VMEM((peers, heads, dim, cols), bf16),
            pltpu.VMEM((peers, heads, dim, cols), bf16),
            pltpu.VMEM((peers, heads, 8, cols), f32),
            pltpu.VMEM((peers, heads, 8, cols), f32),
            pltpu.VMEM((heads, dim, cols), f32),
            dma((chips, heads, chunks)), dma((chips, heads, chunks)),
            dma((chips - 1, heads, chunks)), dma((chips - 1, heads, chunks)),
            dma((tp - 1,)), dma((tp - 1,)),
            dma((peers,)), dma((peers,)),
            dma((peers,)), dma((peers,)),
            dma((peers, heads)), dma((peers, heads)),
            dma((peers, heads)), dma((peers, heads)),
            dma(()),
            dma((blocks_dev,)), dma((blocks_dev,)),
        ],
        compiler_params=pltpu.CompilerParams(
            collective_id=0, has_side_effects=True, vmem_limit_bytes=56 * 1024 * 1024
        ),
    )(
        tokens,
        norm_gain.astype(f32).reshape(1, features),
        kv_weight.reshape(features * all_heads, lanes),
        decode_query.reshape(heads, cols, dim),
        resident_cache,
        new_kv,
        block_owner,
        page_table,
        context_len.reshape(1, requests),
    )
    return out.reshape(heads, requests, group_size, dim)


def solution(mesh):
    sizes = dict(mesh.shape)
    return jax.shard_map(
        functools.partial(per_device, sizes["section"], sizes["tp"]),
        mesh=mesh,
        in_specs=(
            P(("groups", "section"), "tp"),
            P("tp"),
            P("tp", None, None),
            P("groups", None),
            P("tp", ("groups", "section"), None, None),
            P(("groups", "section"), None),
            P(("groups", "section")),
            P("tp", ("groups", "section"), None, None),
            P("tp", ("groups", "section"), None),
        ),
        out_specs=P("tp", ("groups", "section"), None, None),
        check_vma=False,
    )
```

```python
import functools
import math

import jax
import jax.numpy as jnp
from jax import lax
from jax.experimental import pallas as pl
from jax.experimental.pallas import tpu as pltpu
from jax.sharding import PartitionSpec as P

D = 8192


EPSILON = 1e-05
NEG = -1e30
GROUP = 4
MESH = pl.DeviceIdType.MESH


def count_pages(
    sections, heads, pool, block, owner_ref, table_ref, length_ref, full_ref, edge_ref, aux_ref
):
    total_blocks = owner_ref.shape[1]
    blocks_dev = total_blocks // sections
    slots_peer = 2 * ((blocks_dev + sections - 1) // sections)
    depth, requests = table_ref.shape
    cols = full_ref.shape[1]
    me = lax.axis_index("section")
    f32 = jnp.float32

    def iota(shape, axis):
        return lax.broadcasted_iota(jnp.int32, shape, axis)

    grid = (total_blocks, total_blocks)
    along = jnp.broadcast_to(owner_ref[...], grid).astype(f32)
    row, column = iota(grid, 0), iota(grid, 1)
    across = jnp.sum(jnp.where(row == column, along, 0.0), axis=1, keepdims=True)
    earlier = (across == along) & (column < row)
    earlier = earlier & (lax.div(column, blocks_dev) == lax.div(row, blocks_dev))
    rank = jnp.sum(jnp.where(earlier, 1.0, 0.0), axis=1, keepdims=True)
    tall = (total_blocks, 1)
    slot = pool + lax.div(iota(tall, 0), blocks_dev) * slots_peer
    placed = jnp.where(across == me.astype(f32), slot.astype(f32) + rank, -1.0)

    spread = iota((requests, cols), 0) == lax.div(iota((requests, cols), 1), cols // requests)
    spread = jnp.where(spread, 1.0, 0.0)
    columns = jnp.dot(table_ref[...].astype(f32), spread, preferred_element_type=f32)
    length = jnp.broadcast_to(length_ref[...], (8, requests))
    split = lax.div(length, block)
    blocks_held = jnp.dot(split.astype(f32), spread, preferred_element_type=f32)[:1]
    rest = jnp.dot((length - split * block).astype(f32), spread, preferred_element_type=f32)[:1]

    def counts(pages):
        full = jnp.zeros((pages.shape[0], cols), f32)
        edge = jnp.zeros((pages.shape[0], cols), f32)
        for j in range(depth):
            same = jnp.where(pages == columns[j : j + 1], 1.0, 0.0)
            full = full + jnp.where(blocks_held > j, same, 0.0)
            edge = edge + jnp.where(blocks_held == j, same, 0.0)
        return full, edge

    full, edge = counts(iota((pool, 1), 0).astype(f32))
    full_ref[...] = full
    edge_ref[...] = edge
    zeros = (blocks_held * block + rest) - jnp.sum(full * block + edge * rest, axis=0, keepdims=True)
    full, edge = counts(placed)
    zeros = zeros - jnp.sum(full * block + edge * rest, axis=0, keepdims=True)
    for s in range(sections):
        at = slice(s * blocks_dev, (s + 1) * blocks_dev)
        aux_ref[s, :blocks_dev] = full[at]
        aux_ref[s, blocks_dev : 2 * blocks_dev] = edge[at]
        aux_ref[s, 2 * blocks_dev :] = jnp.concatenate(
            [rest, zeros, jnp.zeros((6, cols), f32)], axis=0
        )


def kernel(
    sections, tp, heads, block, chunk,
    part_ref, token_ref, query_ref, cache_ref, fresh_ref, owner_ref, table_ref, length_ref,
    out_ref,
    tokens, sq_ref, full_ref, edge_ref, aux_ref,
    sib, cross_out, cross_in, sq_in, query_in, aux_in, kv, pages, scores, acc, res_acc,
    back_out, back_in, stat_out, stat_in, own_acc,
    sib_s, sib_r, cross_s, cross_r, sq_s, sq_r, query_s, query_r, aux_s, aux_r,
    back_s, back_r, stat_s, stat_r, page_s, token_s,
):
    me = lax.axis_index("section")
    t = lax.axis_index("tp")
    core, x = lax.rem(t, 2), lax.div(t, 2)
    chips = tp // 2
    rows = part_ref.shape[1]
    chunks = rows // chunk
    cols = query_ref.shape[1]
    dim = query_ref.shape[2]
    pool = cache_ref.shape[1]
    blocks_dev = rows // block
    scale = 1.0 / math.sqrt(dim)

    barrier = pltpu.get_barrier_semaphore()
    for d in range(1, tp):
        pl.semaphore_signal(
            barrier, inc=1, device_id={"tp": lax.rem(t + d, tp)}, device_id_type=MESH
        )
    for d in range(1, sections):
        pl.semaphore_signal(
            barrier, inc=1, device_id={"section": lax.rem(me + d, sections)}, device_id_type=MESH
        )
    pl.semaphore_wait(barrier, tp + sections - 2)

    def span(i):
        return pl.ds(pl.multiple_of(i * chunk, chunk), chunk)

    def sib_copy(d, h, i):
        group = lax.rem(x + d, chips) * 2 + 1 - core
        return pltpu.make_async_remote_copy(
            src_ref=part_ref.at[group * heads + h, span(i)],
            dst_ref=sib.at[d, h, span(i)],
            send_sem=sib_s.at[d, h, i],
            recv_sem=sib_r.at[d, h, i],
            device_id={"tp": x * 2 + 1 - core},
            device_id_type=MESH,
        )

    def cross_copy(d, h, i):
        return pltpu.make_async_remote_copy(
            src_ref=cross_out.at[d - 1, h, span(i)],
            dst_ref=cross_in.at[d - 1, h, span(i)],
            send_sem=cross_s.at[d - 1, h, i],
            recv_sem=cross_r.at[d - 1, h, i],
            device_id={"tp": lax.rem(x + d, chips) * 2 + core},
            device_id_type=MESH,
        )

    def sq_copy(d):
        return pltpu.make_async_remote_copy(
            src_ref=sq_ref,
            dst_ref=sq_in.at[d - 1],
            send_sem=sq_s.at[d - 1],
            recv_sem=sq_r.at[d - 1],
            device_id={"tp": lax.rem(t + d, tp)},
            device_id_type=MESH,
        )

    def query_copy(d):
        return pltpu.make_async_remote_copy(
            src_ref=query_ref,
            dst_ref=query_in.at[d - 1],
            send_sem=query_s.at[d - 1],
            recv_sem=query_r.at[d - 1],
            device_id={"section": lax.rem(me + d, sections)},
            device_id_type=MESH,
        )

    def aux_copy(d):
        peer = lax.rem(me + d, sections)
        return pltpu.make_async_remote_copy(
            src_ref=aux_ref.at[peer],
            dst_ref=aux_in.at[d - 1],
            send_sem=aux_s.at[d - 1],
            recv_sem=aux_r.at[d - 1],
            device_id={"section": peer},
            device_id_type=MESH,
        )

    def back_copy(d, h):
        return pltpu.make_async_remote_copy(
            src_ref=back_out.at[d - 1, h],
            dst_ref=back_in.at[d - 1, h],
            send_sem=back_s.at[d - 1, h],
            recv_sem=back_r.at[d - 1, h],
            device_id={"section": lax.rem(me + sections - d, sections)},
            device_id_type=MESH,
        )

    def stat_copy(d, h):
        return pltpu.make_async_remote_copy(
            src_ref=stat_out.at[d - 1, h],
            dst_ref=stat_in.at[d - 1, h],
            send_sem=stat_s.at[d - 1, h],
            recv_sem=stat_r.at[d - 1, h],
            device_id={"section": lax.rem(me + sections - d, sections)},
            device_id_type=MESH,
        )

    def page_copy():
        return pltpu.make_async_copy(cache_ref, pages, page_s)

    def token_copy():
        return pltpu.make_async_copy(token_ref, tokens, token_s)

    for h in range(heads):
        for d in range(1, chips):
            for i in range(chunks):
                sib_copy(d, h, i).start()
    token_copy().start()
    page_copy().start()
    for d in range(1, sections):
        query_copy(d).start()

    count_pages(
        sections, heads, pool, block, owner_ref, table_ref, length_ref, full_ref, edge_ref, aux_ref
    )
    for d in range(1, sections):
        aux_copy(d).start()

    def cross(h):
        for d in range(1, chips):
            group = lax.rem(x + d, chips) * 2 + core
            for i in range(chunks):
                sib_copy(d, h, i).wait_recv()
                mine = part_ref[group * heads + h, span(i)]
                theirs = sib[d, h, span(i)]
                cross_out[d - 1, h, span(i)] = (
                    mine.astype(jnp.float32) + theirs.astype(jnp.float32)
                ).astype(jnp.bfloat16)
                if h == 0:
                    cross_copy(d, h, i).start()

    for h in range(heads):
        cross(h)
    for h in range(heads):
        for i in range(chunks):
            sib_copy(0, h, i).start()

    token_copy().wait()

    def square(j, carry):
        total = jnp.zeros((block, 128), jnp.float32)
        at = pl.ds(pl.multiple_of(j * block, block), block)
        for k in range(tokens.shape[1] // 128):
            piece = tokens[at, k * 128 : (k + 1) * 128].astype(jnp.float32)
            total = total + piece * piece
        sq_ref[pl.ds(j, 1), :] = jnp.sum(jnp.transpose(total), axis=0, keepdims=True)
        return carry

    lax.fori_loop(0, blocks_dev, square, 0)
    for d in range(1, tp):
        sq_copy(d).start()

    position = lax.broadcasted_iota(jnp.int32, (block, cols), 0).astype(jnp.float32)

    def attend(query, load, count_rows, rest, n_pages, extra=None, zeros=None):
        inside = position < rest

        def count(p):
            full, edge = count_rows(p)
            return full + jnp.where(inside, edge, 0.0)

        def first(step, top):
            base = step * GROUP
            for k in range(GROUP):
                keys = load(base + k)[:, :dim]
                s = lax.dot_general(
                    keys, query, (((1,), (1,)), ((), ())), preferred_element_type=jnp.float32
                ) * scale
                s = jnp.where(count(base + k) > 0, s, NEG)
                scores[pl.ds(pl.multiple_of((base + k) * block, block), block)] = s
                top = jnp.maximum(top, jnp.max(s.reshape(block // 8, 8, cols), axis=0))
            return top

        top = lax.fori_loop(0, n_pages // GROUP, first, jnp.full((8, cols), NEG, jnp.float32))
        top = jnp.max(top, axis=0, keepdims=True)
        if extra is not None:
            fresh = extra
            requests = fresh.shape[0]
            own = (
                lax.broadcasted_iota(jnp.int32, (requests, cols), 0) * (cols // requests)
            )
            column = lax.broadcasted_iota(jnp.int32, (requests, cols), 1)
            own = (column >= own) & (column < own + cols // requests)
            s_own = lax.dot_general(
                fresh[:, :dim], query, (((1,), (1,)), ((), ())), preferred_element_type=jnp.float32
            ) * scale
            s_own = jnp.where(own, s_own, NEG)
            top = jnp.maximum(top, jnp.max(s_own, axis=0, keepdims=True))
            top = jnp.maximum(top, jnp.where(zeros > 0, 0.0, NEG))
            w_own = jnp.where(own, jnp.exp(s_own - top), 0.0)
            acc[...] = lax.dot_general(
                fresh[:, dim:], w_own.astype(jnp.bfloat16), (((0,), (0,)), ((), ())),
                preferred_element_type=jnp.float32,
            )
            total = jnp.sum(w_own, axis=0, keepdims=True)
            total = total + jnp.where(zeros > 0, zeros * jnp.exp(0.0 - top), 0.0)
        else:
            acc[...] = jnp.zeros_like(acc)
            total = jnp.zeros((1, cols), jnp.float32)

        def second(step, total8):
            base = step * GROUP
            values, lows = [], []
            for k in range(GROUP):
                s = scores[pl.ds(pl.multiple_of((base + k) * block, block), block)]
                w = jnp.exp(s - top)
                c = count(base + k)
                total8 = total8 + jnp.sum((w * c).reshape(block // 8, 8, cols), axis=0)
                low = w.astype(jnp.bfloat16).astype(jnp.float32) * c
                lows.append(low.astype(jnp.bfloat16))
                values.append(load(base + k)[:, dim:])
            acc[...] += lax.dot_general(
                jnp.concatenate(values, axis=0), jnp.concatenate(lows, axis=0),
                (((0,), (0,)), ((), ())), preferred_element_type=jnp.float32,
            )
            return total8

        total8 = lax.fori_loop(0, n_pages // GROUP, second, jnp.zeros((8, cols), jnp.float32))
        return top, total + jnp.sum(total8, axis=0, keepdims=True)

    page_copy().wait()
    rest_own = aux_ref[0, 2 * blocks_dev : 2 * blocks_dev + 1, :]
    zeros_own = aux_ref[0, 2 * blocks_dev + 1 : 2 * blocks_dev + 2, :]
    res_stats = []
    for h in range(heads):
        stat = attend(
            query_ref[h],
            lambda p, h=h: pages[h, p],
            lambda p: (full_ref[pl.ds(p, 1), :], edge_ref[pl.ds(p, 1), :]),
            rest_own,
            pool,
            fresh_ref[h],
            zeros_own,
        )
        res_stats.append(stat)
        res_acc[h] = acc[...]

    for d in range(1, tp):
        sq_copy(d).wait_recv()
    squares = sq_ref[...]
    for d in range(1, tp):
        squares = squares + sq_in[d - 1]
    inverse = lax.rsqrt(squares / D + EPSILON)
    diagonal = lax.broadcasted_iota(jnp.int32, (block, block), 0) == lax.broadcasted_iota(
        jnp.int32, (block, block), 1
    )
    per_chunk = chunk // block

    def load_block(h):
        return lambda p: kv[h, pl.ds(pl.multiple_of(p * block, block), block)]

    for h in range(heads):
        if h + 1 < heads:
            for d in range(1, chips):
                for i in range(chunks):
                    cross_copy(d, h, i).wait_send()
            for d in range(1, chips):
                for i in range(chunks):
                    cross_copy(d, h + 1, i).start()
        for i in range(chunks):
            sib_copy(0, h, i).wait_recv()
            for d in range(1, chips):
                cross_copy(d, h, i).wait_recv()
            for k in range(per_chunk):
                j = i * per_chunk + k
                lanes = inverse[j : j + 1, :]
                factor = jnp.sum(
                    jnp.where(diagonal, jnp.broadcast_to(lanes, (block, block)), 0.0),
                    axis=1,
                    keepdims=True,
                )
                at = slice(j * block, (j + 1) * block)
                value = part_ref[t * heads + h, at].astype(jnp.float32) + sib[0, h, at].astype(
                    jnp.float32
                )
                for d in range(1, chips):
                    value = value + cross_in[d - 1, h, at].astype(jnp.float32)
                kv[h, at] = (value * factor).astype(jnp.bfloat16)

        def serve(d, carry, h=h):
            if h == 0:
                query_copy(d).wait_recv()
                aux_copy(d).wait_recv()
            top, total = attend(
                query_in[d - 1, h],
                load_block(h),
                lambda p: (
                    aux_in[d - 1, pl.ds(p, 1), :],
                    aux_in[d - 1, pl.ds(blocks_dev + p, 1), :],
                ),
                aux_in[d - 1, 2 * blocks_dev : 2 * blocks_dev + 1, :],
                blocks_dev,
            )
            back_out[d - 1, h] = acc[...].astype(jnp.bfloat16)
            stat_out[d - 1, h] = jnp.concatenate(
                [top, total, jnp.zeros((6, cols), jnp.float32)], axis=0
            )
            back_copy(d, h).start()
            stat_copy(d, h).start()
            return carry

        lax.fori_loop(1, sections, serve, 0)

    own_stats = []
    for h in range(heads):
        stat = attend(
            query_ref[h],
            load_block(h),
            lambda p: (
                aux_ref[me, pl.ds(p, 1), :],
                aux_ref[me, pl.ds(blocks_dev + p, 1), :],
            ),
            rest_own,
            blocks_dev,
        )
        own_stats.append(stat)
        own_acc[h] = acc[...]

    for h in range(heads):
        for d in range(1, sections):
            back_copy(d, h).wait_recv()
            stat_copy(d, h).wait_recv()
        tops = [res_stats[h][0], own_stats[h][0]]
        totals = [res_stats[h][1], own_stats[h][1]]
        for d in range(1, sections):
            tops.append(stat_in[d - 1, h, 0:1, :])
            totals.append(stat_in[d - 1, h, 1:2, :])
        top = functools.reduce(jnp.maximum, tops)
        factors = [jnp.exp(one - top) for one in tops]
        total = sum(f * one for f, one in zip(factors, totals))
        mixed = res_acc[h] * factors[0] + own_acc[h] * factors[1]
        for d in range(1, sections):
            mixed = mixed + back_in[d - 1, h].astype(jnp.float32) * factors[d + 1]
        out_ref[h] = jnp.transpose(mixed / total)

    for h in range(heads):
        for i in range(chunks):
            for d in range(chips):
                sib_copy(d, h, i).wait_send()
                if d and h == heads - 1:
                    cross_copy(d, h, i).wait_send()
    for d in range(1, tp):
        sq_copy(d).wait_send()
    for d in range(1, sections):
        query_copy(d).wait_send()
        aux_copy(d).wait_send()
        for h in range(heads):
            back_copy(d, h).wait_send()
            stat_copy(d, h).wait_send()


def per_device(
    sections,
    tp,
    tokens,
    norm_gain,
    kv_weight,
    block_owner,
    resident_cache,
    page_table,
    context_len,
    decode_query,
    new_kv,
):
    heads, pool, block, lanes = resident_cache.shape
    _, requests, group_size, dim = decode_query.shape
    cols = requests * group_size
    rows = tokens.shape[0]
    blocks_dev = rows // block
    chunk = min(rows, 512)
    chunks = rows // chunk
    chips = tp // 2
    widened = tokens.astype(jnp.float32)
    normed = (widened * norm_gain.astype(jnp.float32)[None, :]).astype(jnp.bfloat16)
    part = jnp.einsum(
        "td,dhc->htc", normed, kv_weight, preferred_element_type=jnp.float32
    ).astype(jnp.bfloat16)
    aux_rows = 2 * blocks_dev + 8
    vmem = pl.BlockSpec(memory_space=pltpu.VMEM)
    anywhere = pl.BlockSpec(memory_space=pl.ANY)
    dma = pltpu.SemaphoreType.DMA
    peers = sections - 1
    bf16, f32 = jnp.bfloat16, jnp.float32
    out = pl.pallas_call(
        functools.partial(kernel, sections, tp, heads, block, chunk),
        out_shape=jax.ShapeDtypeStruct((heads, cols, dim), f32),
        in_specs=[vmem, anywhere, vmem, anywhere, vmem, vmem, vmem, vmem],
        out_specs=vmem,
        scratch_shapes=[
            pltpu.VMEM(tokens.shape, bf16),
            pltpu.VMEM((blocks_dev, block), f32),
            pltpu.VMEM((pool, cols), f32),
            pltpu.VMEM((pool, cols), f32),
            pltpu.VMEM((sections, aux_rows, cols), f32),
            pltpu.VMEM((chips, heads, rows, lanes), bf16),
            pltpu.VMEM((chips - 1, heads, rows, lanes), bf16),
            pltpu.VMEM((chips - 1, heads, rows, lanes), bf16),
            pltpu.VMEM((tp - 1, blocks_dev, block), f32),
            pltpu.VMEM((peers, heads, cols, dim), bf16),
            pltpu.VMEM((peers, aux_rows, cols), f32),
            pltpu.VMEM((heads, rows, lanes), bf16),
            pltpu.VMEM((heads, pool, block, lanes), bf16),
            pltpu.VMEM((max(pool, blocks_dev) * block, cols), f32),
            pltpu.VMEM((dim, cols), f32),
            pltpu.VMEM((heads, dim, cols), f32),
            pltpu.VMEM((peers, heads, dim, cols), bf16),
            pltpu.VMEM((peers, heads, dim, cols), bf16),
            pltpu.VMEM((peers, heads, 8, cols), f32),
            pltpu.VMEM((peers, heads, 8, cols), f32),
            pltpu.VMEM((heads, dim, cols), f32),
            dma((chips, heads, chunks)), dma((chips, heads, chunks)),
            dma((chips - 1, heads, chunks)), dma((chips - 1, heads, chunks)),
            dma((tp - 1,)), dma((tp - 1,)),
            dma((peers,)), dma((peers,)),
            dma((peers,)), dma((peers,)),
            dma((peers, heads)), dma((peers, heads)),
            dma((peers, heads)), dma((peers, heads)),
            dma(()),
            dma(()),
        ],
        compiler_params=pltpu.CompilerParams(
            collective_id=0, has_side_effects=True, vmem_limit_bytes=48 * 1024 * 1024
        ),
    )(
        part,
        tokens,
        decode_query.reshape(heads, cols, dim),
        resident_cache,
        new_kv,
        block_owner.reshape(1, -1),
        page_table.T,
        context_len.reshape(1, requests),
    )
    return out.reshape(heads, requests, group_size, dim)


def solution(mesh):
    sizes = dict(mesh.shape)
    return jax.shard_map(
        functools.partial(per_device, sizes["section"], sizes["tp"]),
        mesh=mesh,
        in_specs=(
            P(("groups", "section"), "tp"),
            P("tp"),
            P("tp", None, None),
            P("groups", None),
            P("tp", ("groups", "section"), None, None),
            P(("groups", "section"), None),
            P(("groups", "section")),
            P("tp", ("groups", "section"), None, None),
            P("tp", ("groups", "section"), None),
        ),
        out_specs=P("tp", ("groups", "section"), None, None),
        check_vma=False,
    )
```

```python
import functools
import math

import jax
import jax.numpy as jnp
from jax import lax
from jax.experimental import pallas as pl
from jax.experimental.pallas import tpu as pltpu
from jax.sharding import PartitionSpec as P

D = 8192


EPSILON = 1e-05
NEG = -1e30
GROUP = 4
MESH = pl.DeviceIdType.MESH


def count_pages(
    sections, heads, pool, block, owner_ref, table_ref, length_ref, full_ref, edge_ref, aux_ref
):
    total_blocks = owner_ref.shape[1]
    blocks_dev = total_blocks // sections
    slots_peer = 2 * ((blocks_dev + sections - 1) // sections)
    depth, requests = table_ref.shape
    cols = full_ref.shape[1]
    me = lax.axis_index("section")
    f32 = jnp.float32

    def iota(shape, axis):
        return lax.broadcasted_iota(jnp.int32, shape, axis)

    grid = (total_blocks, total_blocks)
    along = jnp.broadcast_to(owner_ref[...], grid).astype(f32)
    row, column = iota(grid, 0), iota(grid, 1)
    across = jnp.sum(jnp.where(row == column, along, 0.0), axis=1, keepdims=True)
    earlier = (across == along) & (column < row)
    earlier = earlier & (lax.div(column, blocks_dev) == lax.div(row, blocks_dev))
    rank = jnp.sum(jnp.where(earlier, 1.0, 0.0), axis=1, keepdims=True)
    tall = (total_blocks, 1)
    slot = pool + lax.div(iota(tall, 0), blocks_dev) * slots_peer
    placed = jnp.where(across == me.astype(f32), slot.astype(f32) + rank, -1.0)

    spread = iota((requests, cols), 0) == lax.div(iota((requests, cols), 1), cols // requests)
    spread = jnp.where(spread, 1.0, 0.0)
    columns = jnp.dot(table_ref[...].astype(f32), spread, preferred_element_type=f32)
    length = jnp.broadcast_to(length_ref[...], (8, requests))
    split = lax.div(length, block)
    blocks_held = jnp.dot(split.astype(f32), spread, preferred_element_type=f32)[:1]
    rest = jnp.dot((length - split * block).astype(f32), spread, preferred_element_type=f32)[:1]

    def counts(pages):
        full = jnp.zeros((pages.shape[0], cols), f32)
        edge = jnp.zeros((pages.shape[0], cols), f32)
        for j in range(depth):
            same = jnp.where(pages == columns[j : j + 1], 1.0, 0.0)
            full = full + jnp.where(blocks_held > j, same, 0.0)
            edge = edge + jnp.where(blocks_held == j, same, 0.0)
        return full, edge

    full, edge = counts(iota((pool, 1), 0).astype(f32))
    full_ref[...] = full
    edge_ref[...] = edge
    zeros = (blocks_held * block + rest) - jnp.sum(full * block + edge * rest, axis=0, keepdims=True)
    full, edge = counts(placed)
    zeros = zeros - jnp.sum(full * block + edge * rest, axis=0, keepdims=True)
    for s in range(sections):
        at = slice(s * blocks_dev, (s + 1) * blocks_dev)
        aux_ref[s, :blocks_dev] = full[at]
        aux_ref[s, blocks_dev : 2 * blocks_dev] = edge[at]
        aux_ref[s, 2 * blocks_dev :] = jnp.concatenate(
            [rest, zeros, jnp.zeros((6, cols), f32)], axis=0
        )


def kernel(
    sections, tp, heads, block, chunk,
    part_ref, token_ref, query_ref, cache_ref, fresh_ref, owner_ref, table_ref, length_ref,
    out_ref,
    tokens, sq_ref, full_ref, edge_ref, aux_ref,
    sib, cross_out, cross_in, sq_in, query_in, aux_in, kv, pages, scores, acc, res_acc,
    back_out, back_in, stat_out, stat_in, own_acc,
    sib_s, sib_r, cross_s, cross_r, sq_s, sq_r, query_s, query_r, aux_s, aux_r,
    back_s, back_r, stat_s, stat_r, page_s, token_s,
):
    me = lax.axis_index("section")
    t = lax.axis_index("tp")
    core, x = lax.rem(t, 2), lax.div(t, 2)
    chips = tp // 2
    rows = part_ref.shape[1]
    chunks = rows // chunk
    cols = query_ref.shape[1]
    dim = query_ref.shape[2]
    pool = cache_ref.shape[1]
    blocks_dev = rows // block
    scale = 1.0 / math.sqrt(dim)

    barrier = pltpu.get_barrier_semaphore()
    for d in range(1, tp):
        pl.semaphore_signal(
            barrier, inc=1, device_id={"tp": lax.rem(t + d, tp)}, device_id_type=MESH
        )
    for d in range(1, sections):
        pl.semaphore_signal(
            barrier, inc=1, device_id={"section": lax.rem(me + d, sections)}, device_id_type=MESH
        )
    pl.semaphore_wait(barrier, tp + sections - 2)

    def span(i):
        return pl.ds(pl.multiple_of(i * chunk, chunk), chunk)

    def sib_copy(d, h, i):
        group = lax.rem(x + d, chips) * 2 + 1 - core
        return pltpu.make_async_remote_copy(
            src_ref=part_ref.at[group * heads + h, span(i)],
            dst_ref=sib.at[d, h, span(i)],
            send_sem=sib_s.at[d, h, i],
            recv_sem=sib_r.at[d, h, i],
            device_id={"tp": x * 2 + 1 - core},
            device_id_type=MESH,
        )

    def cross_copy(d, h, i):
        return pltpu.make_async_remote_copy(
            src_ref=cross_out.at[d - 1, h, span(i)],
            dst_ref=cross_in.at[d - 1, h, span(i)],
            send_sem=cross_s.at[d - 1, h, i],
            recv_sem=cross_r.at[d - 1, h, i],
            device_id={"tp": lax.rem(x + d, chips) * 2 + core},
            device_id_type=MESH,
        )

    def sq_copy(d):
        return pltpu.make_async_remote_copy(
            src_ref=sq_ref,
            dst_ref=sq_in.at[d - 1],
            send_sem=sq_s.at[d - 1],
            recv_sem=sq_r.at[d - 1],
            device_id={"tp": lax.rem(t + d, tp)},
            device_id_type=MESH,
        )

    def query_copy(d):
        return pltpu.make_async_remote_copy(
            src_ref=query_ref,
            dst_ref=query_in.at[d - 1],
            send_sem=query_s.at[d - 1],
            recv_sem=query_r.at[d - 1],
            device_id={"section": lax.rem(me + d, sections)},
            device_id_type=MESH,
        )

    def aux_copy(d):
        peer = lax.rem(me + d, sections)
        return pltpu.make_async_remote_copy(
            src_ref=aux_ref.at[peer],
            dst_ref=aux_in.at[d - 1],
            send_sem=aux_s.at[d - 1],
            recv_sem=aux_r.at[d - 1],
            device_id={"section": peer},
            device_id_type=MESH,
        )

    def back_copy(d, h):
        return pltpu.make_async_remote_copy(
            src_ref=back_out.at[d - 1, h],
            dst_ref=back_in.at[d - 1, h],
            send_sem=back_s.at[d - 1, h],
            recv_sem=back_r.at[d - 1, h],
            device_id={"section": lax.rem(me + sections - d, sections)},
            device_id_type=MESH,
        )

    def stat_copy(d, h):
        return pltpu.make_async_remote_copy(
            src_ref=stat_out.at[d - 1, h],
            dst_ref=stat_in.at[d - 1, h],
            send_sem=stat_s.at[d - 1, h],
            recv_sem=stat_r.at[d - 1, h],
            device_id={"section": lax.rem(me + sections - d, sections)},
            device_id_type=MESH,
        )

    def page_copy():
        return pltpu.make_async_copy(cache_ref, pages, page_s)

    def token_copy():
        return pltpu.make_async_copy(token_ref, tokens, token_s)

    for h in range(heads):
        for d in range(1, chips):
            for i in range(chunks):
                sib_copy(d, h, i).start()
    token_copy().start()
    page_copy().start()
    for d in range(1, sections):
        query_copy(d).start()

    count_pages(
        sections, heads, pool, block, owner_ref, table_ref, length_ref, full_ref, edge_ref, aux_ref
    )
    for d in range(1, sections):
        aux_copy(d).start()

    def cross(h):
        for d in range(1, chips):
            group = lax.rem(x + d, chips) * 2 + core
            for i in range(chunks):
                sib_copy(d, h, i).wait_recv()
                mine = part_ref[group * heads + h, span(i)]
                theirs = sib[d, h, span(i)]
                cross_out[d - 1, h, span(i)] = (
                    mine.astype(jnp.float32) + theirs.astype(jnp.float32)
                ).astype(jnp.bfloat16)
                if h == 0:
                    cross_copy(d, h, i).start()

    for h in range(heads):
        cross(h)
    for h in range(heads):
        for i in range(chunks):
            sib_copy(0, h, i).start()

    token_copy().wait()

    def square(j, carry):
        total = jnp.zeros((block, 128), jnp.float32)
        at = pl.ds(pl.multiple_of(j * block, block), block)
        for k in range(tokens.shape[1] // 128):
            piece = tokens[at, k * 128 : (k + 1) * 128].astype(jnp.float32)
            total = total + piece * piece
        sq_ref[pl.ds(j, 1), :] = jnp.sum(jnp.transpose(total), axis=0, keepdims=True)
        return carry

    lax.fori_loop(0, blocks_dev, square, 0)
    for d in range(1, tp):
        sq_copy(d).start()

    position = lax.broadcasted_iota(jnp.int32, (block, cols), 0).astype(jnp.float32)

    def attend(query, load, count_rows, rest, n_pages, extra=None, zeros=None):
        inside = position < rest

        def count(p):
            full, edge = count_rows(p)
            return full + jnp.where(inside, edge, 0.0)

        def first(step, top):
            base = step * GROUP
            for k in range(GROUP):
                keys = load(base + k)[:, :dim]
                s = lax.dot_general(
                    keys, query, (((1,), (1,)), ((), ())), preferred_element_type=jnp.float32
                ) * scale
                s = jnp.where(count(base + k) > 0, s, NEG)
                scores[pl.ds(pl.multiple_of((base + k) * block, block), block)] = s
                top = jnp.maximum(top, jnp.max(s.reshape(block // 8, 8, cols), axis=0))
            return top

        top = lax.fori_loop(0, n_pages // GROUP, first, jnp.full((8, cols), NEG, jnp.float32))
        top = jnp.max(top, axis=0, keepdims=True)
        if extra is not None:
            fresh = extra
            requests = fresh.shape[0]
            own = (
                lax.broadcasted_iota(jnp.int32, (requests, cols), 0) * (cols // requests)
            )
            column = lax.broadcasted_iota(jnp.int32, (requests, cols), 1)
            own = (column >= own) & (column < own + cols // requests)
            s_own = lax.dot_general(
                fresh[:, :dim], query, (((1,), (1,)), ((), ())), preferred_element_type=jnp.float32
            ) * scale
            s_own = jnp.where(own, s_own, NEG)
            top = jnp.maximum(top, jnp.max(s_own, axis=0, keepdims=True))
            top = jnp.maximum(top, jnp.where(zeros > 0, 0.0, NEG))
            w_own = jnp.where(own, jnp.exp(s_own - top), 0.0)
            acc[...] = lax.dot_general(
                fresh[:, dim:], w_own.astype(jnp.bfloat16), (((0,), (0,)), ((), ())),
                preferred_element_type=jnp.float32,
            )
            total = jnp.sum(w_own, axis=0, keepdims=True)
            total = total + jnp.where(zeros > 0, zeros * jnp.exp(0.0 - top), 0.0)
        else:
            acc[...] = jnp.zeros_like(acc)
            total = jnp.zeros((1, cols), jnp.float32)

        def second(step, total8):
            base = step * GROUP
            values, lows = [], []
            for k in range(GROUP):
                s = scores[pl.ds(pl.multiple_of((base + k) * block, block), block)]
                w = jnp.exp(s - top)
                c = count(base + k)
                total8 = total8 + jnp.sum((w * c).reshape(block // 8, 8, cols), axis=0)
                low = w.astype(jnp.bfloat16).astype(jnp.float32) * c
                lows.append(low.astype(jnp.bfloat16))
                values.append(load(base + k)[:, dim:])
            acc[...] += lax.dot_general(
                jnp.concatenate(values, axis=0), jnp.concatenate(lows, axis=0),
                (((0,), (0,)), ((), ())), preferred_element_type=jnp.float32,
            )
            return total8

        total8 = lax.fori_loop(0, n_pages // GROUP, second, jnp.zeros((8, cols), jnp.float32))
        return top, total + jnp.sum(total8, axis=0, keepdims=True)

    page_copy().wait()
    rest_own = aux_ref[0, 2 * blocks_dev : 2 * blocks_dev + 1, :]
    zeros_own = aux_ref[0, 2 * blocks_dev + 1 : 2 * blocks_dev + 2, :]
    res_stats = []
    for h in range(heads):
        stat = attend(
            query_ref[h],
            lambda p, h=h: pages[h, p],
            lambda p: (full_ref[pl.ds(p, 1), :], edge_ref[pl.ds(p, 1), :]),
            rest_own,
            pool,
            fresh_ref[h],
            zeros_own,
        )
        res_stats.append(stat)
        res_acc[h] = acc[...]

    for d in range(1, tp):
        sq_copy(d).wait_recv()
    squares = sq_ref[...]
    for d in range(1, tp):
        squares = squares + sq_in[d - 1]
    inverse = lax.rsqrt(squares / D + EPSILON)
    diagonal = lax.broadcasted_iota(jnp.int32, (block, block), 0) == lax.broadcasted_iota(
        jnp.int32, (block, block), 1
    )
    per_chunk = chunk // block

    def load_block(h):
        return lambda p: kv[h, pl.ds(pl.multiple_of(p * block, block), block)]

    for h in range(heads):
        if h + 1 < heads:
            for d in range(1, chips):
                for i in range(chunks):
                    cross_copy(d, h, i).wait_send()
            for d in range(1, chips):
                for i in range(chunks):
                    cross_copy(d, h + 1, i).start()
        for i in range(chunks):
            sib_copy(0, h, i).wait_recv()
            for d in range(1, chips):
                cross_copy(d, h, i).wait_recv()
            for k in range(per_chunk):
                j = i * per_chunk + k
                lanes = inverse[j : j + 1, :]
                factor = jnp.sum(
                    jnp.where(diagonal, jnp.broadcast_to(lanes, (block, block)), 0.0),
                    axis=1,
                    keepdims=True,
                )
                at = slice(j * block, (j + 1) * block)
                value = part_ref[t * heads + h, at].astype(jnp.float32) + sib[0, h, at].astype(
                    jnp.float32
                )
                for d in range(1, chips):
                    value = value + cross_in[d - 1, h, at].astype(jnp.float32)
                kv[h, at] = (value * factor).astype(jnp.bfloat16)

        def serve(d, carry, h=h):
            if h == 0:
                query_copy(d).wait_recv()
                aux_copy(d).wait_recv()
            top, total = attend(
                query_in[d - 1, h],
                load_block(h),
                lambda p: (
                    aux_in[d - 1, pl.ds(p, 1), :],
                    aux_in[d - 1, pl.ds(blocks_dev + p, 1), :],
                ),
                aux_in[d - 1, 2 * blocks_dev : 2 * blocks_dev + 1, :],
                blocks_dev,
            )
            back_out[d - 1, h] = acc[...].astype(jnp.bfloat16)
            stat_out[d - 1, h] = jnp.concatenate(
                [top, total, jnp.zeros((6, cols), jnp.float32)], axis=0
            )
            back_copy(d, h).start()
            stat_copy(d, h).start()
            return carry

        lax.fori_loop(1, sections, serve, 0)

    own_stats = []
    for h in range(heads):
        stat = attend(
            query_ref[h],
            load_block(h),
            lambda p: (
                aux_ref[me, pl.ds(p, 1), :],
                aux_ref[me, pl.ds(blocks_dev + p, 1), :],
            ),
            rest_own,
            blocks_dev,
        )
        own_stats.append(stat)
        own_acc[h] = acc[...]

    for h in range(heads):
        for d in range(1, sections):
            back_copy(d, h).wait_recv()
            stat_copy(d, h).wait_recv()
        tops = [res_stats[h][0], own_stats[h][0]]
        totals = [res_stats[h][1], own_stats[h][1]]
        for d in range(1, sections):
            tops.append(stat_in[d - 1, h, 0:1, :])
            totals.append(stat_in[d - 1, h, 1:2, :])
        top = functools.reduce(jnp.maximum, tops)
        factors = [jnp.exp(one - top) for one in tops]
        total = sum(f * one for f, one in zip(factors, totals))
        mixed = res_acc[h] * factors[0] + own_acc[h] * factors[1]
        for d in range(1, sections):
            mixed = mixed + back_in[d - 1, h].astype(jnp.float32) * factors[d + 1]
        out_ref[h] = jnp.transpose(mixed / total)

    for h in range(heads):
        for i in range(chunks):
            for d in range(chips):
                sib_copy(d, h, i).wait_send()
                if d and h == heads - 1:
                    cross_copy(d, h, i).wait_send()
    for d in range(1, tp):
        sq_copy(d).wait_send()
    for d in range(1, sections):
        query_copy(d).wait_send()
        aux_copy(d).wait_send()
        for h in range(heads):
            back_copy(d, h).wait_send()
            stat_copy(d, h).wait_send()


def per_device(
    sections,
    tp,
    tokens,
    norm_gain,
    kv_weight,
    block_owner,
    resident_cache,
    page_table,
    context_len,
    decode_query,
    new_kv,
):
    heads, pool, block, lanes = resident_cache.shape
    _, requests, group_size, dim = decode_query.shape
    cols = requests * group_size
    rows = tokens.shape[0]
    blocks_dev = rows // block
    chunk = min(rows, 512)
    chunks = rows // chunk
    chips = tp // 2
    normed = tokens * norm_gain[None, :]
    part = jnp.einsum(
        "td,dhc->htc", normed, kv_weight, preferred_element_type=jnp.float32
    ).astype(jnp.bfloat16)
    aux_rows = 2 * blocks_dev + 8
    vmem = pl.BlockSpec(memory_space=pltpu.VMEM)
    anywhere = pl.BlockSpec(memory_space=pl.ANY)
    dma = pltpu.SemaphoreType.DMA
    peers = sections - 1
    bf16, f32 = jnp.bfloat16, jnp.float32
    out = pl.pallas_call(
        functools.partial(kernel, sections, tp, heads, block, chunk),
        out_shape=jax.ShapeDtypeStruct((heads, cols, dim), f32),
        in_specs=[vmem, anywhere, vmem, anywhere, vmem, vmem, vmem, vmem],
        out_specs=vmem,
        scratch_shapes=[
            pltpu.VMEM(tokens.shape, bf16),
            pltpu.VMEM((blocks_dev, block), f32),
            pltpu.VMEM((pool, cols), f32),
            pltpu.VMEM((pool, cols), f32),
            pltpu.VMEM((sections, aux_rows, cols), f32),
            pltpu.VMEM((chips, heads, rows, lanes), bf16),
            pltpu.VMEM((chips - 1, heads, rows, lanes), bf16),
            pltpu.VMEM((chips - 1, heads, rows, lanes), bf16),
            pltpu.VMEM((tp - 1, blocks_dev, block), f32),
            pltpu.VMEM((peers, heads, cols, dim), bf16),
            pltpu.VMEM((peers, aux_rows, cols), f32),
            pltpu.VMEM((heads, rows, lanes), bf16),
            pltpu.VMEM((heads, pool, block, lanes), bf16),
            pltpu.VMEM((max(pool, blocks_dev) * block, cols), f32),
            pltpu.VMEM((dim, cols), f32),
            pltpu.VMEM((heads, dim, cols), f32),
            pltpu.VMEM((peers, heads, dim, cols), bf16),
            pltpu.VMEM((peers, heads, dim, cols), bf16),
            pltpu.VMEM((peers, heads, 8, cols), f32),
            pltpu.VMEM((peers, heads, 8, cols), f32),
            pltpu.VMEM((heads, dim, cols), f32),
            dma((chips, heads, chunks)), dma((chips, heads, chunks)),
            dma((chips - 1, heads, chunks)), dma((chips - 1, heads, chunks)),
            dma((tp - 1,)), dma((tp - 1,)),
            dma((peers,)), dma((peers,)),
            dma((peers,)), dma((peers,)),
            dma((peers, heads)), dma((peers, heads)),
            dma((peers, heads)), dma((peers, heads)),
            dma(()),
            dma(()),
        ],
        compiler_params=pltpu.CompilerParams(
            collective_id=0, has_side_effects=True, vmem_limit_bytes=48 * 1024 * 1024
        ),
    )(
        part,
        tokens,
        decode_query.reshape(heads, cols, dim),
        resident_cache,
        new_kv,
        block_owner.reshape(1, -1),
        page_table.T,
        context_len.reshape(1, requests),
    )
    return out.reshape(heads, requests, group_size, dim)


def solution(mesh):
    sizes = dict(mesh.shape)
    return jax.shard_map(
        functools.partial(per_device, sizes["section"], sizes["tp"]),
        mesh=mesh,
        in_specs=(
            P(("groups", "section"), "tp"),
            P("tp"),
            P("tp", None, None),
            P("groups", None),
            P("tp", ("groups", "section"), None, None),
            P(("groups", "section"), None),
            P(("groups", "section")),
            P("tp", ("groups", "section"), None, None),
            P("tp", ("groups", "section"), None),
        ),
        out_specs=P("tp", ("groups", "section"), None, None),
        check_vma=False,
    )
```
